128 devices in a mesh: ctx: 8 (over z, y_hi), tp: 16 (over y_lo, x, core).
Axes of the slice: x: 4, y: 4 (y_hi: 2, y_lo: 2; y = y_hi * 2 + y_lo), z: 4, core: 2. Of those that a mesh axis runs over, the one named last changes fastest.
Arguments:
- queries: bfloat16 [4096, 12288], P('ctx', 'tp'), may hold values from -10 to 10
- kv_latent: bfloat16 [4096, 512], P(('ctx', 'tp')), may hold values from -6 to 6
- key_rope: bfloat16 [4096, 64], P(('ctx', 'tp')), may hold values from -6 to 6
- w_key: bfloat16 [512, 8192], P(None, 'tp'), may hold values from -0.25 to 0.25
- w_value: bfloat16 [512, 8192], P(None, 'tp'), may hold values from -0.25 to 0.25
- w_out: bfloat16 [8192, 2560], P('tp'), may hold values from -0.25 to 0.25
- residual: bfloat16 [4096, 2560], P(('ctx', 'tp')), may hold values from -36 to 36
- moe_gain: float32 [2560], replicated, may hold values from 0.5 to 1.5
- shared_gate: bfloat16 [2560, 3072], P(None, 'tp'), may hold values from -0.125 to 0.125
- shared_up: bfloat16 [2560, 3072], P(None, 'tp'), may hold values from -0.125 to 0.125
- shared_down: bfloat16 [3072, 2560], P('tp'), may hold values from -0.109375 to 0.109375
- expert_gate_up: bfloat16 [128, 2560, 1536], P(('ctx', 'tp')), may hold values from -0.125 to 0.125
- expert_down: bfloat16 [128, 768, 2560], P(('ctx', 'tp')), may hold values from -0.21875 to 0.21875
- expert_ids: int32 [4096, 6], P(('ctx', 'tp')), may hold values from 0 to 127, all different within a row; in each aligned block of 32 rows (0 to 31, 32 to 63, ...) at most 3 rows name the same one
- gate_weights: float32 [4096, 6], P(('ctx', 'tp')), may hold values from 0.1 to 0.6
Outputs:
- layer_out: bfloat16 [4096, 2560], P(('ctx', 'tp'))
The draws below stay inside these ranges and needn't reach their ends.
Inputs may be any that keep to these rules, and one draw needn't show every extreme that they name: `expert_ids`: each row names 6 different experts; among the rows that one device holds no expert is named more than 3 times, and on some device one expert is named exactly 3 times; every expert is named somewhere.
All inputs are finite; a program needn't handle non-finite values.
Results may differ from the reference program's by a relative error of at most 0.022.
Values may be sent and summed in bfloat16 or wider, within the bound.
A program may use at most 128 MiB of HBM per device.

```python
import math
import jax
import jax.numpy as jnp
import numpy as np
from jax import lax

D = 2560
HEADS = 64
NOPE = 128
ROPE = 64
VDIM = 128
LATENT = 512
FF_E = 768
SHARED = 3072
TOPK = 6
SEQ_DEV = 512
LENGTH = 4096
EXPERTS = 128
CAP = 3
N_CTX = 8
N_TP = 16


def draw_queries(key, part):
    key = jax.random.fold_in(key, 12)
    all_width = HEADS * (NOPE + ROPE)
    drawn = jnp.clip(2.0 * jax.random.normal(key, (LENGTH, all_width), jnp.float32), -6.0, 6.0)
    return drawn.astype(jnp.bfloat16)


def draw_key_rope(key, part):
    key = jax.random.fold_in(key, 11)
    drawn = jnp.clip(jax.random.normal(key, (LENGTH, ROPE), jnp.float32), -4.0, 4.0)
    return drawn.astype(jnp.bfloat16)


def draw_residual(key, part):
    key = jax.random.fold_in(key, 13)
    row_key = jax.random.fold_in(key, 1)
    col_key = jax.random.fold_in(key, 2)
    base_key = jax.random.fold_in(key, 3)
    row_scale = jnp.exp(jax.random.uniform(row_key, (LENGTH, 1), jnp.float32, math.log(0.3), math.log(3.0)))
    col_scale = jnp.exp(jax.random.uniform(col_key, (1, D), jnp.float32, math.log(0.3), math.log(3.0)))
    base_values = jnp.clip(jax.random.normal(base_key, (LENGTH, D), jnp.float32), -4.0, 4.0)
    return (base_values * row_scale * col_scale).astype(jnp.bfloat16)


def level_of(own_key, extent, pieces, smallest, largest):
    def one(axis_at, blocks):
        heights = jax.random.uniform(jax.random.fold_in(jax.random.fold_in(own_key, 6), axis_at), (blocks,), jnp.float32, smallest / len(pieces), largest / len(pieces))
        return jnp.repeat(jnp.exp(heights), extent[axis_at] // blocks).reshape((-1,) + (1,) * (len(extent) - axis_at - 1))

    loudness = one(*pieces[0])
    for cut in pieces[1:]:
        loudness = loudness * one(*cut)
    return loudness


def shared_out(rng, own, number, rows, amount, top, bound, slope):
    order = jax.random.permutation(rng, amount)
    heavy_load, usual = load_shares(amount, rows * top, bound, slope, True), load_shares(amount, rows * top, bound, slope, False)
    places = jnp.arange(amount)

    def named(sizes, rotation):
        used = int((sizes > 0).sum())
        fixed = max(1, used // 4)
        passed = fixed + (places - fixed + rotation * (used - fixed)) % max(1, amount - fixed)
        return jnp.zeros((amount,), jnp.int32).at[order[jnp.where(places < fixed, places, passed)]].set(jnp.asarray(sizes, jnp.int32))

    sizes = jnp.where(number % 4 == 0, named(heavy_load, number // 4), named(usual, number - number // 4 - 1))
    mixed = jax.random.permutation(jax.random.fold_in(own, 3), amount)
    giver, receiver = mixed[0:amount // 2 * 2:2], mixed[1:amount // 2 * 2:2]
    room = jnp.minimum(sizes[giver] - 1, bound - sizes[receiver]) // 2
    room = jnp.where((giver == order[0]) | (receiver == order[0]) | (sizes[receiver] == 0), 0, jnp.maximum(room, 0))
    passed = jax.random.randint(jax.random.fold_in(own, 4), (amount // 2,), 0, 1 << 20) % (room + 1)
    sizes = sizes.at[giver].add(-passed).at[receiver].add(passed)
    items = jnp.searchsorted(jnp.cumsum(sizes), jnp.arange(rows * top), side="right").astype(jnp.int32)
    grid = items.reshape(top, rows).T
    grid = grid[jax.random.permutation(jax.random.fold_in(own, 1), rows)]
    rotation = jax.random.randint(jax.random.fold_in(own, 2), (rows, 1), 0, top)
    return jnp.take_along_axis(grid, (jnp.arange(top)[None, :] + rotation) % top, axis=1)


def load_shares(count, total, limit, slope, full):
    loads = [(1 << 20) // math.isqrt(grade ** slope) + 1 for grade in range(1, count + 1)]
    largest = limit if full else min(limit, max(-(-total // count), total * loads[0] // sum(loads)))
    least = 1 if total - largest >= count - 1 else 0
    counts, spare = [largest] + [least] * (count - 1), total - largest - least * (count - 1)
    while spare > 0:
        free = [i for i in range(1, count) if counts[i] < largest] or [i for i in range(1, count) if counts[i] < limit]
        mass, left = sum([loads[i] for i in free]), spare
        for i in free:
            extra = min(limit - counts[i], max(1, left * loads[i] // mass), spare)
            counts[i] = counts[i] + extra
            spare = spare - extra
    return np.array(counts)


def scatter_about(stream_key, dims, width, most, split=(), kind=jnp.bfloat16):
    result = width * jax.random.normal(stream_key, dims, jnp.float32)
    if split:
        result = result * level_of(stream_key, dims, split, -0.22, 0.18)
    return jnp.clip(result, -most, most).astype(kind)


def setup_inputs(seed: int = 0) -> dict:
    arg_keys = jax.random.split(jax.random.key(seed), 16)
    queries = draw_queries(jax.random.fold_in(arg_keys[15], 71), 0)
    kv_latent = scatter_about(arg_keys[1], (LENGTH, LATENT), 1.0, 6.0, ((0, 128),))
    key_rope = draw_key_rope(jax.random.fold_in(arg_keys[15], 71), 0)
    w_key = scatter_about(arg_keys[3], (LATENT, HEADS * NOPE), LATENT ** -0.5, 0.25, ((1, 16),))
    w_value = scatter_about(arg_keys[4], (LATENT, HEADS * VDIM), LATENT ** -0.5, 0.25, ((1, 16),))
    w_out = scatter_about(arg_keys[5], (HEADS * VDIM, D), (HEADS * VDIM // 16) ** -0.5, 0.25, ((0, 16),))
    residual = draw_residual(jax.random.fold_in(arg_keys[15], 71), 0)
    moe_gain = jnp.clip(jax.random.uniform(arg_keys[7], (D,), jnp.float32, 0.5, 1.5), 0.5, 1.5)
    shared_gate = scatter_about(arg_keys[8], (D, SHARED), D ** -0.5, 0.125, ((1, 16),))
    shared_up = scatter_about(arg_keys[9], (D, SHARED), D ** -0.5, 0.125, ((1, 16),))
    shared_down = scatter_about(arg_keys[10], (SHARED, D), SHARED ** -0.5, 0.109375, ((0, 16),))
    expert_gate_up = scatter_about(arg_keys[11], (EXPERTS, D, 2 * FF_E), D ** -0.5, 0.125, ((0, 128),))
    expert_down = scatter_about(arg_keys[12], (EXPERTS, FF_E, D), FF_E ** -0.5, 0.21875, ((0, 128),))
    expert_ids_keys = jax.random.split(jax.random.fold_in(arg_keys[13], 1), LENGTH // (SEQ_DEV // N_TP))
    expert_ids_turns = jax.random.permutation(jax.random.fold_in(arg_keys[13], 3), LENGTH // (SEQ_DEV // N_TP))
    expert_ids = jax.vmap(lambda own, number: shared_out(jax.random.fold_in(arg_keys[13], 2), own, number, SEQ_DEV // N_TP, EXPERTS, TOPK, CAP, 2))(expert_ids_keys, expert_ids_turns).reshape((LENGTH, TOPK))
    gate_weights = jnp.clip(0.1 + 0.5 * jax.random.uniform(arg_keys[14], (LENGTH, TOPK), jnp.float32) ** level_of(arg_keys[14], (LENGTH, TOPK), ((0, 128),), -0.2, 0.2), 0.1, 0.6)
    return {"queries": queries, "kv_latent": kv_latent, "key_rope": key_rope, "w_key": w_key, "w_value": w_value, "w_out": w_out, "residual": residual, "moe_gain": moe_gain, "shared_gate": shared_gate, "shared_up": shared_up, "shared_down": shared_down, "expert_gate_up": expert_gate_up, "expert_down": expert_down, "expert_ids": expert_ids, "gate_weights": gate_weights}


def attend_head(query_head, key_map, value_map, kv_latent, key_rope):
    key_nope = jnp.dot(kv_latent, key_map, preferred_element_type=jnp.float32).astype(jnp.bfloat16)
    values = jnp.dot(kv_latent, value_map, preferred_element_type=jnp.float32).astype(jnp.bfloat16)
    score_scale = 1.0 / math.sqrt(NOPE + ROPE)
    outputs = []
    for block_index in range(N_CTX):
        first_row = block_index * SEQ_DEV
        end_row = first_row + SEQ_DEV
        query_rows = query_head[first_row:end_row]
        scores = jnp.dot(query_rows[:, :NOPE], key_nope[:end_row].T, preferred_element_type=jnp.float32)
        scores = scores + jnp.dot(query_rows[:, NOPE:], key_rope[:end_row].T, preferred_element_type=jnp.float32)
        scores = scores * score_scale
        query_position = first_row + jnp.arange(SEQ_DEV, dtype=jnp.int32)
        key_position = jnp.arange(end_row, dtype=jnp.int32)
        visible = key_position[None, :] <= query_position[:, None]
        row_top = lax.optimization_barrier(jnp.max(jnp.where(visible, scores, -jnp.inf), axis=1, keepdims=True))
        weights = jnp.where(visible, jnp.exp(scores - row_top), 0.0)
        totals = lax.optimization_barrier(jnp.sum(weights, axis=1, keepdims=True))
        weights_low = weights.astype(jnp.bfloat16)
        output = jnp.dot(weights_low, values[:end_row], preferred_element_type=jnp.float32) / totals
        outputs.append(output.astype(jnp.bfloat16))
    return jnp.concatenate(outputs, axis=0)

def expert_scan(normed, expert_gate_up, expert_down, expert_ids, gate_weights):
    flat_experts = expert_ids.reshape(-1)
    flat_gates = gate_weights.reshape(-1)
    slot_room = N_CTX * N_TP * CAP

    def one_expert(routed, expert_args):
        expert_index, gate_up, down_map = expert_args
        chosen = flat_experts == expert_index
        picked_rows = jnp.nonzero(chosen, size=slot_room, fill_value=0)[0].astype(jnp.int32)
        filled = jnp.arange(slot_room, dtype=jnp.int32) < jnp.sum(chosen.astype(jnp.int32))
        token_index = (picked_rows // TOPK).astype(jnp.int32)
        token_rows = normed[token_index]
        gate_up_part = jnp.dot(token_rows, gate_up, preferred_element_type=jnp.float32)
        expert_hidden = (jax.nn.silu(gate_up_part[:, :FF_E]) * gate_up_part[:, FF_E:]).astype(jnp.bfloat16)
        expert_output = jnp.dot(expert_hidden, down_map, preferred_element_type=jnp.float32).astype(jnp.bfloat16)
        gate_share = jnp.where(filled, flat_gates[picked_rows], 0.0)
        routed = routed.at[token_index].add(gate_share[:, None] * expert_output.astype(jnp.float32))
        return (routed, gate_share)
    initial = jnp.zeros(normed.shape, jnp.float32)
    expert_range = jnp.arange(EXPERTS, dtype=jnp.int32)
    return lax.scan(one_expert, initial, (expert_range, expert_gate_up, expert_down))[0]

def reference(queries, kv_latent, key_rope, w_key, w_value, w_out, residual, moe_gain, shared_gate, shared_up, shared_down, expert_gate_up, expert_down, expert_ids, gate_weights):
    length = queries.shape[0]
    query_heads = queries.reshape(length, HEADS, NOPE + ROPE).transpose(1, 0, 2)
    key_maps = w_key.reshape(LATENT, HEADS, NOPE).transpose(1, 0, 2)
    value_maps = w_value.reshape(LATENT, HEADS, VDIM).transpose(1, 0, 2)

    def one_head(head_args):
        return attend_head(head_args[0], head_args[1], head_args[2], kv_latent, key_rope)
    per_head = lax.map(one_head, (query_heads, key_maps, value_maps))
    attention = per_head.transpose(1, 0, 2).reshape(length, HEADS * VDIM)
    hidden_state = residual.astype(jnp.float32) + jnp.dot(attention, w_out, preferred_element_type=jnp.float32)
    mean_square = lax.optimization_barrier(jnp.mean(hidden_state * hidden_state, axis=1, keepdims=True))
    normed = (hidden_state * lax.rsqrt(mean_square + 1e-06) * moe_gain).astype(jnp.bfloat16)
    gate_part = jnp.dot(normed, shared_gate, preferred_element_type=jnp.float32)
    up_part = jnp.dot(normed, shared_up, preferred_element_type=jnp.float32)
    shared_hidden = (jax.nn.silu(gate_part) * up_part).astype(jnp.bfloat16)
    shared_output = jnp.dot(shared_hidden, shared_down, preferred_element_type=jnp.float32)
    routed = expert_scan(normed, expert_gate_up, expert_down, expert_ids, gate_weights)
    return (hidden_state + shared_output + routed).astype(jnp.bfloat16)
```

```python
import functools
import math

import jax
import jax.numpy as jnp
from jax import lax
from jax.experimental import pallas as pl
from jax.experimental.pallas import tpu as pltpu
from jax.sharding import PartitionSpec as P

NOPE = 128
ROPE = 64
VDIM = 128
TOPK = 6
CAP = 3
MESH = pl.DeviceIdType.MESH
F32 = jnp.float32
BF16 = jnp.bfloat16
LOW = -1e30
CHUNKS = 5


def loop(first, end, body):
    def step(i, carry):
        body(i)
        return carry

    lax.fori_loop(first, end, step, 0)


def dot(a, b):
    return jnp.dot(a, b, preferred_element_type=F32)


def layer_kernel(
    tail_ref,
    queries,
    w_key,
    w_value,
    w_out_hbm,
    residual,
    gain,
    shared_gate_hbm,
    shared_up_hbm,
    shared_down_hbm,
    gate_up_hbm,
    down_hbm,
    out_ref,
    w_out,
    shared_gate,
    shared_up,
    shared_down,
    gate_up,
    down,
    load_sem,
    lat,
    q_s,
    k_s,
    v_s,
    top_s,
    acc_s,
    lat_ctx_send,
    lat_ctx_recv,
    lat_tp_send,
    lat_tp_recv,
    lat_sib_send,
    lat_sib_recv,
    part,
    sib_in,
    row_in,
    a_sib_send,
    a_sib_recv,
    a_row_send,
    a_row_recv,
    hidden,
    normed,
    n_send,
    n_recv,
    n_sib_send,
    n_sib_recv,
    pick,
    give,
    slots_out,
    slots_in,
    up_acc,
    x_send,
    x_recv,
    back_out,
    back_in,
    y_send,
    y_recv,
    shared_acc,
    part2,
    sib_in2,
    row_in2,
    b_sib_send,
    b_sib_recv,
    b_row_send,
    b_row_recv,
):
    c = lax.axis_index("ctx")
    t = lax.axis_index("tp")
    chip = t // 2
    core = t % 2
    other = 1 - core
    sibling = (c, chip * 2 + other)
    rows = residual.shape[0]
    width = residual.shape[1]
    heads = q_s.shape[0]
    latent = w_key.shape[0]
    n_ctx, _, n_chip = lat.shape[:3]
    half = n_chip * rows
    group = 2 * half
    span = width // CHUNKS
    slot_room = slots_out.shape[1]

    def cols(n):
        return pl.ds(n * span, span)

    def remote(src, dst, send, recv, device):
        return pltpu.make_async_remote_copy(
            src_ref=src,
            dst_ref=dst,
            send_sem=send,
            recv_sem=recv,
            device_id=device,
            device_id_type=MESH,
        )

    def chip_at(d):
        j = (chip + d) % n_chip
        return j, (c, j * 2 + core)

    def ctx_at(d):
        j = (c + d) % n_ctx
        return j, (j, t)

    loads = []
    for i, (src, dst) in enumerate(
        (
            (w_out_hbm, w_out),
            (shared_gate_hbm, shared_gate),
            (shared_up_hbm, shared_up),
            (shared_down_hbm, shared_down),
            (gate_up_hbm.at[0], gate_up),
            (down_hbm.at[0], down),
        )
    ):
        load = pltpu.make_async_copy(src, dst, load_sem.at[i])
        load.start()
        loads.append(load)

    barrier = pltpu.get_barrier_semaphore()

    def greet(device):
        pl.semaphore_signal(barrier, inc=1, device_id=device, device_id_type=MESH)

    loop(1, n_chip, lambda d: greet(chip_at(d)[1]))
    loop(1, n_ctx, lambda d: greet(ctx_at(d)[1]))
    greet(sibling)
    pl.semaphore_wait(barrier, n_chip + n_ctx - 1)

    lat[c, core, chip] = tail_ref[...]

    def ctx_copy(s, j, d):
        return remote(
            lat.at[s, core, chip],
            lat.at[s, core, chip],
            lat_ctx_send.at[d],
            lat_ctx_recv.at[s],
            (j, t),
        )

    loop(1, n_ctx - c, lambda d: ctx_copy(c, c + d, d).start())

    def tp_copy(s, d):
        _, device = chip_at(d)
        return remote(
            lat.at[s, core, chip],
            lat.at[s, core, chip],
            lat_tp_send.at[s, d],
            lat_tp_recv.at[s, chip],
            device,
        )

    def tp_wait(s, d):
        j, device = chip_at(d)
        remote(
            lat.at[s, core, j],
            lat.at[s, core, j],
            lat_tp_send.at[s, d],
            lat_tp_recv.at[s, j],
            device,
        ).wait_recv()

    loop(1, n_chip, lambda d: tp_copy(c, d).start())

    q_all = queries[...].reshape(n_chip, 2, rows, queries.shape[1])
    for k in range(2):
        q_half = q_all[:, k].reshape(half, queries.shape[1])
        for h in range(heads):
            piece = q_half[:, h * (NOPE + ROPE) : (h + 1) * (NOPE + ROPE)]
            q_s[h, k * half : (k + 1) * half, :] = jnp.concatenate(
                [piece, jnp.zeros((half, 2 * NOPE - NOPE - ROPE), BF16)], axis=1
            )
    top_s[...] = jnp.full(top_s.shape, LOW, F32)
    acc_s[...] = jnp.zeros(acc_s.shape, F32)

    def pass_on(i):
        s = c - i
        ctx_copy(s, (c + 1) % n_ctx, 0).wait_recv()
        loop(1, n_chip, lambda d: tp_copy(s, d).start())

    loop(1, c + 1, pass_on)

    scale = (1.0 / math.sqrt(NOPE + ROPE)) * math.log2(math.e)

    def place(index, axis_shape, axis):
        i = lax.broadcasted_iota(jnp.int32, axis_shape, axis) + index
        return ((i & (half - 1)) // rows) * (2 * rows) + (i // half) * rows + (i & (rows - 1))

    def attend(s, k, diagonal):
        block = lat[s, k].reshape(half, lat.shape[4])
        k_s[...] = dot(block[:, :latent], w_key[...]).astype(BF16)
        v_s[...] = dot(block[:, :latent], w_value[...]).astype(BF16)
        rope = block[:, latent:]
        ones = jnp.ones((half, VDIM), BF16)
        for h in range(heads):
            keys = jnp.concatenate([k_s[:, h * NOPE : (h + 1) * NOPE], rope], axis=1)
            values = jnp.concatenate([v_s[:, h * VDIM : (h + 1) * VDIM], ones], axis=1)
            scores = lax.dot_general(
                q_s[h], keys, (((1,), (1,)), ((), ())), preferred_element_type=F32
            )
            if diagonal:
                query_at = place(0, (group, half), 0)
                key_at = place(k * half, (group, half), 1)
                scores = jnp.where(key_at <= query_at, scores, LOW)
            top_old = top_s[h]
            top_new = jnp.maximum(top_old, jnp.max(scores, axis=1, keepdims=True))
            top_s[h] = top_new
            weights = jnp.concatenate(
                [
                    jnp.exp2((scores[:, j * 128 : (j + 1) * 128] - top_new) * scale).astype(BF16)
                    for j in range(half // 128)
                ],
                axis=1,
            )
            factor = jnp.exp2((top_old - top_new) * scale)
            factor = jnp.concatenate([factor, factor], axis=1)
            acc_s[h] = acc_s[h] * factor + dot(weights, values)

    def sib_copy(s, k):
        return remote(lat.at[s, k], lat.at[s, k], lat_sib_send.at[s], lat_sib_recv.at[s], sibling)

    def key_step(i, diagonal):
        s = c - i
        loop(1, n_chip, lambda d: tp_wait(s, d))
        sib_copy(s, core).start()

        def half_step(j):
            @pl.when(j == 1)
            def _():
                sib_copy(s, other).wait_recv()

            attend(s, (core + j) % 2, diagonal)

        loop(0, 2, half_step)

    key_step(0, True)
    loop(1, c + 1, lambda i: key_step(i, False))

    def sib_part(n, buffer, landing, send, recv, k):
        return remote(
            buffer.at[k, :, :, cols(n)],
            landing.at[:, :, cols(n)],
            send.at[n],
            recv.at[n],
            sibling,
        )

    def row_part(n, d, buffer, landing, send, recv):
        j, device = chip_at(d)
        return remote(
            buffer.at[core, j, :, cols(n)],
            landing.at[chip, :, cols(n)],
            send.at[n, d],
            recv.at[n, chip],
            device,
        )

    def row_wait(n, d, buffer, landing, send, recv):
        j, device = chip_at(d)
        remote(
            buffer.at[core, j, :, cols(n)],
            landing.at[j, :, cols(n)],
            send.at[n, d],
            recv.at[n, j],
            device,
        ).wait_recv()

    def pass_rows(n, buffer, from_sibling, landing, sib_send, sib_recv, send, recv):
        sib_part(n, buffer, from_sibling, sib_send, sib_recv, other).wait_recv()
        summed = (
            buffer[core, :, :, cols(n)].astype(F32) + from_sibling[:, :, cols(n)].astype(F32)
        ).astype(BF16)
        buffer[core, :, :, cols(n)] = summed
        landing[chip, :, cols(n)] = buffer[core, chip, :, cols(n)]
        loop(1, n_chip, lambda d: row_part(n, d, buffer, landing, send, recv).start())

    def sum_rows(n, buffer, landing, send, recv):
        loop(1, n_chip, lambda d: row_wait(n, d, buffer, landing, send, recv))
        return jnp.sum(landing[:, :, cols(n)].astype(F32), axis=0)

    attention = jnp.concatenate(
        [(acc_s[h, :, :VDIM] / acc_s[h, :, VDIM:]).astype(BF16) for h in range(heads)], axis=1
    )
    loads[0].wait()
    first = (part, sib_in, row_in, a_sib_send, a_sib_recv, a_row_send, a_row_recv)
    for n in range(CHUNKS):
        part[:, :, :, cols(n)] = (
            dot(attention, w_out[:, cols(n)]).astype(BF16).reshape(2, n_chip, rows, span)
        )
        sib_part(n, part, sib_in, a_sib_send, a_sib_recv, other).start()
        if n > 0:
            pass_rows(n - 1, *first)
    pass_rows(CHUNKS - 1, *first)

    meta = lat[c, :, :, :, latent:].reshape(group, lat.shape[4] - latent).astype(F32).T
    ids = meta[ROPE : ROPE + TOPK]
    gates_high = meta[ROPE + 8 : ROPE + 8 + TOPK]
    gates_low = meta[ROPE + 16 : ROPE + 16 + TOPK]
    expert_row = lax.broadcasted_iota(jnp.int32, (16, group), 0)
    expert = jnp.where(expert_row < n_ctx, expert_row * (2 * n_chip) + t, -1).astype(F32)
    member = jnp.zeros((16, group), F32)
    gate = jnp.zeros((16, group), F32)
    for k in range(TOPK):
        same = ids[k : k + 1] == expert
        member = member + jnp.where(same, 1.0, 0.0)
        gate = gate + jnp.where(same, gates_high[k : k + 1] + gates_low[k : k + 1], 0.0)
    before = lax.broadcasted_iota(jnp.int32, (group, group), 0) < lax.broadcasted_iota(
        jnp.int32, (group, group), 1
    )
    rank = dot(member.astype(BF16), jnp.where(before, 1.0, 0.0).astype(BF16))
    slot = lax.broadcasted_iota(jnp.int32, (slot_room, group), 0).astype(F32)
    for e in range(n_ctx):
        chosen = jnp.where(member[e : e + 1] > 0.5, rank[e : e + 1], -1.0) == slot
        pick[e] = jnp.where(chosen, 1.0, 0.0).astype(BF16)
        give[e] = jnp.where(chosen, gate[e : e + 1], 0.0).astype(BF16)

    for n in range(CHUNKS):
        hidden[:, cols(n)] = residual[:, cols(n)].astype(F32) + sum_rows(
            n, part, row_in, a_row_send, a_row_recv
        )
    state = hidden[...]
    mean_square = jnp.mean(state * state, axis=1, keepdims=True)
    normed[core, chip] = (state * lax.rsqrt(mean_square + 1e-06) * gain[...]).astype(BF16)

    def normed_copy(n, d, j):
        _, device = chip_at(d)
        return remote(
            normed.at[core, j, :, cols(n)],
            normed.at[core, j, :, cols(n)],
            n_send.at[n, d],
            n_recv.at[n, j],
            device,
        )

    def normed_sib(n, k):
        return remote(
            normed.at[k, :, :, cols(n)],
            normed.at[k, :, :, cols(n)],
            n_sib_send.at[n],
            n_sib_recv.at[n],
            sibling,
        )

    for n in range(CHUNKS):
        loop(1, n_chip, lambda d: normed_copy(n, d, chip).start())

    def slot_copy(n, d, source, landing, send, recv):
        j, device = ctx_at(d)
        return remote(
            source.at[j, :, cols(n)], landing.at[c, :, cols(n)], send.at[n, d], recv.at[n, c], device
        )

    def slot_wait(n, d, source, landing, send, recv):
        j, device = ctx_at(d)
        remote(
            source.at[j, :, cols(n)], landing.at[j, :, cols(n)], send.at[n, d], recv.at[n, j], device
        ).wait_recv()

    for n in range(CHUNKS):
        loop(1, n_chip, lambda d: normed_copy(n, d, chip_at(d)[0]).wait_recv())
        normed_sib(n, core).start()
        normed_sib(n, other).wait_recv()
        block = normed[:, :, :, cols(n)].reshape(group, span)
        picked = dot(pick[...].reshape(n_ctx * slot_room, group), block).astype(BF16)
        slots_out[:, :, cols(n)] = picked.reshape(n_ctx, slot_room, span)
        loop(1, n_ctx, lambda d: slot_copy(n, d, slots_out, slots_in, x_send, x_recv).start())
        slots_in[c, :, cols(n)] = slots_out[c, :, cols(n)]

    loads[1].wait()
    loads[2].wait()
    everyone = normed[...].reshape(group, width)
    gate_part = dot(everyone, shared_gate[...])
    up_part = dot(everyone, shared_up[...])
    shared_hidden = (gate_part / (1.0 + jnp.exp(-gate_part)) * up_part).astype(BF16)
    loads[3].wait()
    for n in range(CHUNKS):
        shared_acc[:, cols(n)] = dot(shared_hidden, shared_down[:, cols(n)])

    loads[4].wait()
    loads[5].wait()
    for n in range(CHUNKS):
        loop(1, n_ctx, lambda d: slot_wait(n, d, slots_out, slots_in, x_send, x_recv))
        items = slots_in[:, :, cols(n)].reshape(n_ctx * slot_room, span)
        product = dot(items, gate_up[cols(n), :])
        if n == 0:
            up_acc[...] = product
        else:
            up_acc[...] = up_acc[...] + product
    inner = down.shape[0]
    gate_part = up_acc[:, :inner]
    expert_hidden = (gate_part / (1.0 + jnp.exp(-gate_part)) * up_acc[:, inner:]).astype(BF16)
    for n in range(CHUNKS):
        result = dot(expert_hidden, down[:, cols(n)]).astype(BF16)
        back_out[:, :, cols(n)] = result.reshape(n_ctx, slot_room, span)
        loop(1, n_ctx, lambda d: slot_copy(n, d, back_out, back_in, y_send, y_recv).start())
        back_in[c, :, cols(n)] = back_out[c, :, cols(n)]

    give_rows = give[...].reshape(n_ctx * slot_room, group).astype(F32).T.astype(BF16)
    second = (part2, sib_in2, row_in2, b_sib_send, b_sib_recv, b_row_send, b_row_recv)
    for n in range(CHUNKS):
        loop(1, n_ctx, lambda d: slot_wait(n, d, back_out, back_in, y_send, y_recv))
        returned = back_in[:, :, cols(n)].reshape(n_ctx * slot_room, span)
        both = shared_acc[:, cols(n)] + dot(give_rows, returned)
        part2[:, :, :, cols(n)] = both.astype(BF16).reshape(2, n_chip, rows, span)
        sib_part(n, part2, sib_in2, b_sib_send, b_sib_recv, other).start()
        if n > 0:
            pass_rows(n - 1, *second)
    pass_rows(CHUNKS - 1, *second)
    for n in range(CHUNKS):
        out_ref[:, cols(n)] = (
            hidden[:, cols(n)] + sum_rows(n, part2, row_in2, b_row_send, b_row_recv)
        ).astype(BF16)

    loop(1, n_ctx - c, lambda d: ctx_copy(c, c + d, d).wait_send())

    def lat_sent(i):
        loop(1, n_chip, lambda d: tp_copy(c - i, d).wait_send())
        sib_copy(c - i, core).wait_send()

    loop(0, c + 1, lat_sent)
    for n in range(CHUNKS):
        sib_part(n, part, sib_in, a_sib_send, a_sib_recv, other).wait_send()
        sib_part(n, part2, sib_in2, b_sib_send, b_sib_recv, other).wait_send()
        normed_sib(n, core).wait_send()

        def sent(d):
            row_part(n, d, part, row_in, a_row_send, a_row_recv).wait_send()
            row_part(n, d, part2, row_in2, b_row_send, b_row_recv).wait_send()
            normed_copy(n, d, chip).wait_send()

        def slots_sent(d):
            slot_copy(n, d, slots_out, slots_in, x_send, x_recv).wait_send()
            slot_copy(n, d, back_out, back_in, y_send, y_recv).wait_send()

        loop(1, n_chip, sent)
        loop(1, n_ctx, slots_sent)


def shards(
    n_ctx,
    n_tp,
    queries,
    kv_latent,
    key_rope,
    w_key,
    w_value,
    w_out,
    residual,
    moe_gain,
    shared_gate,
    shared_up,
    shared_down,
    expert_gate_up,
    expert_down,
    expert_ids,
    gate_weights,
):
    rows, width = residual.shape
    n_chip = n_tp // 2
    heads = w_key.shape[1] // NOPE
    group = rows * n_tp
    latent = kv_latent.shape[1]
    slot_room = CAP * n_tp
    high = gate_weights.astype(BF16)
    low = (gate_weights - high.astype(F32)).astype(BF16)
    gap = jnp.zeros((rows, 8 - TOPK), BF16)
    row_tail = jnp.concatenate(
        [kv_latent, key_rope, expert_ids.astype(BF16), gap, high, gap, low, gap]
        + [jnp.zeros((rows, 128 - ROPE - 24), BF16)],
        axis=1,
    )
    dma = pltpu.SemaphoreType.DMA
    scratch = [
        pltpu.VMEM(w_out.shape, BF16),
        pltpu.VMEM(shared_gate.shape, BF16),
        pltpu.VMEM(shared_up.shape, BF16),
        pltpu.VMEM(shared_down.shape, BF16),
        pltpu.VMEM(expert_gate_up.shape[1:], BF16),
        pltpu.VMEM(expert_down.shape[1:], BF16),
        dma((6,)),
        pltpu.VMEM((n_ctx, 2, n_chip, rows, latent + 128), BF16),
        pltpu.VMEM((heads, group, 2 * NOPE), BF16),
        pltpu.VMEM((group // 2, heads * NOPE), BF16),
        pltpu.VMEM((group // 2, heads * VDIM), BF16),
        pltpu.VMEM((heads, group, 128), F32),
        pltpu.VMEM((heads, group, 2 * VDIM), F32),
        dma((n_ctx,)),
        dma((n_ctx,)),
        dma((n_ctx, n_chip)),
        dma((n_ctx, n_chip)),
        dma((n_ctx,)),
        dma((n_ctx,)),
        pltpu.VMEM((2, n_chip, rows, width), BF16),
        pltpu.VMEM((n_chip, rows, width), BF16),
        pltpu.VMEM((n_chip, rows, width), BF16),
        dma((CHUNKS,)),
        dma((CHUNKS,)),
        dma((CHUNKS, n_chip)),
        dma((CHUNKS, n_chip)),
        pltpu.VMEM((rows, width), F32),
        pltpu.VMEM((2, n_chip, rows, width), BF16),
        dma((CHUNKS, n_chip)),
        dma((CHUNKS, n_chip)),
        dma((CHUNKS,)),
        dma((CHUNKS,)),
        pltpu.VMEM((n_ctx, slot_room, group), BF16),
        pltpu.VMEM((n_ctx, slot_room, group), BF16),
        pltpu.VMEM((n_ctx, slot_room, width), BF16),
        pltpu.VMEM((n_ctx, slot_room, width), BF16),
        pltpu.VMEM((n_ctx * slot_room, expert_gate_up.shape[2]), F32),
        dma((CHUNKS, n_ctx)),
        dma((CHUNKS, n_ctx)),
        pltpu.VMEM((n_ctx, slot_room, width), BF16),
        pltpu.VMEM((n_ctx, slot_room, width), BF16),
        dma((CHUNKS, n_ctx)),
        dma((CHUNKS, n_ctx)),
        pltpu.VMEM((group, width), F32),
        pltpu.VMEM((2, n_chip, rows, width), BF16),
        pltpu.VMEM((n_chip, rows, width), BF16),
        pltpu.VMEM((n_chip, rows, width), BF16),
        dma((CHUNKS,)),
        dma((CHUNKS,)),
        dma((CHUNKS, n_chip)),
        dma((CHUNKS, n_chip)),
    ]
    vmem = pl.BlockSpec(memory_space=pltpu.VMEM)
    hbm = pl.BlockSpec(memory_space=pl.ANY)
    return pl.pallas_call(
        layer_kernel,
        out_shape=jax.ShapeDtypeStruct((rows, width), BF16),
        in_specs=[vmem, vmem, vmem, vmem, hbm, vmem, vmem, hbm, hbm, hbm, hbm, hbm],
        out_specs=vmem,
        scratch_shapes=scratch,
        compiler_params=pltpu.CompilerParams(
            collective_id=1, has_side_effects=True, vmem_limit_bytes=63 * 1024 * 1024
        ),
        cost_estimate=pl.CostEstimate(
            flops=20_000_000_000, bytes_accessed=20_000_000, transcendentals=9_000_000
        ),
        name="layer",
    )(
        row_tail,
        queries,
        w_key,
        w_value,
        w_out,
        residual,
        moe_gain.reshape(1, width),
        shared_gate,
        shared_up,
        shared_down,
        expert_gate_up,
        expert_down,
    )


def solution(mesh):
    in_specs = (
        P("ctx", "tp"),
        P(("ctx", "tp"), None),
        P(("ctx", "tp"), None),
        P(None, "tp"),
        P(None, "tp"),
        P("tp", None),
        P(("ctx", "tp"), None),
        P(),
        P(None, "tp"),
        P(None, "tp"),
        P("tp", None),
        P(("ctx", "tp"), None, None),
        P(("ctx", "tp"), None, None),
        P(("ctx", "tp"), None),
        P(("ctx", "tp"), None),
    )
    out_specs = P(("ctx", "tp"), None)
    return jax.shard_map(
        functools.partial(shards, mesh.shape["ctx"], mesh.shape["tp"]),
        mesh=mesh,
        in_specs=in_specs,
        out_specs=out_specs,
        check_vma=False,
    )
```

```python
import functools
import math

import jax
import jax.numpy as jnp
from jax import lax
from jax.experimental import pallas as pl
from jax.experimental.pallas import tpu as pltpu
from jax.sharding import PartitionSpec as P

NOPE = 128
ROPE = 64
VDIM = 128
TOPK = 6
CAP = 3
MESH = pl.DeviceIdType.MESH
F32 = jnp.float32
BF16 = jnp.bfloat16
LOW = -1e30
CHUNKS = 5


def loop(first, end, body):
    if isinstance(first, int) and isinstance(end, int):
        for i in range(first, end):
            body(i)
        return

    def step(i, carry):
        body(i)
        return carry

    lax.fori_loop(first, end, step, 0)


def dot(a, b):
    return jnp.dot(a, b, preferred_element_type=F32)


def dot_rows(a, b):
    return lax.dot_general(a, b, (((1,), (1,)), ((), ())), preferred_element_type=F32)


def layer_kernel(
    queries_hbm,
    kv_latent_hbm,
    key_rope_hbm,
    w_key_hbm,
    w_value_hbm,
    w_out_hbm,
    residual_hbm,
    gain_hbm,
    shared_gate_hbm,
    shared_up_hbm,
    shared_down_hbm,
    gate_up_hbm,
    down_hbm,
    ids_hbm,
    gates_hbm,
    out_ref,
    kv_latent,
    key_rope,
    ids_ref,
    gates_ref,
    queries,
    w_key,
    w_value,
    residual,
    gain,
    w_out,
    shared_gate,
    shared_up,
    shared_down,
    gate_up,
    down,
    load_sem,
    lat,
    q_s,
    k_s,
    v_s,
    top_s,
    acc_s,
    lat_ctx_send,
    lat_ctx_recv,
    lat_tp_send,
    lat_tp_recv,
    lat_sib_send,
    lat_sib_recv,
    part,
    sib_in,
    row_in,
    a_sib_send,
    a_sib_recv,
    a_row_send,
    a_row_recv,
    hidden,
    normed,
    n_send,
    n_recv,
    n_sib_send,
    n_sib_recv,
    pick,
    give,
    slots_out,
    slots_in,
    up_acc,
    x_send,
    x_recv,
    back_out,
    back_in,
    y_send,
    y_recv,
    shared_acc,
    part2,
    sib_in2,
    row_in2,
    b_sib_send,
    b_sib_recv,
    b_row_send,
    b_row_recv,
):
    c = lax.axis_index("ctx")
    t = lax.axis_index("tp")
    chip = t // 2
    core = t % 2
    other = 1 - core
    sibling = (c, chip * 2 + other)
    rows = residual.shape[0]
    width = residual.shape[1]
    heads = q_s.shape[0]
    latent = w_key.shape[0]
    n_ctx, _, n_chip = lat.shape[:3]
    half = n_chip * rows
    group = 2 * half
    span = width // CHUNKS
    slot_room = slots_out.shape[1]

    def cols(n):
        return pl.ds(n * span, span)

    def remote(src, dst, send, recv, device):
        return pltpu.make_async_remote_copy(
            src_ref=src,
            dst_ref=dst,
            send_sem=send,
            recv_sem=recv,
            device_id=device,
            device_id_type=MESH,
        )

    def chip_at(d):
        j = (chip + d) % n_chip
        return j, (c, j * 2 + core)

    def across(j):
        return ((j + c) % 2) * (n_chip // 2)

    def ctx_at(d):
        j = (c + d) % n_ctx
        return j, (j, ((chip + across(j)) % n_chip) * 2 + core)

    loads = []
    for i, (src, dst) in enumerate(
        (
            (kv_latent_hbm, kv_latent),
            (key_rope_hbm, key_rope),
            (ids_hbm, ids_ref),
            (gates_hbm, gates_ref),
            (queries_hbm, queries),
            (w_key_hbm, w_key),
            (w_value_hbm, w_value),
            (residual_hbm, residual),
            (gain_hbm, gain),
            (w_out_hbm, w_out),
            (shared_gate_hbm, shared_gate),
            (shared_up_hbm, shared_up),
            (shared_down_hbm, shared_down),
            (gate_up_hbm.at[0], gate_up),
            (down_hbm.at[0], down),
        )
    ):
        load = pltpu.make_async_copy(src, dst, load_sem.at[i])
        loads.append(load)
    for load in loads[:9]:
        load.start()
    loaded = set()

    def use(i):
        loaded.add(i)
        loads[i].wait()

    pending = []

    def finish():
        for i in range(len(loads)):
            if i not in loaded and (i < 9 or len(pending) > 1 or (pending and i < 10)):
                use(i)
        for wait in pending:
            wait()

    barrier = pltpu.get_barrier_semaphore()

    def greet(device):
        pl.semaphore_signal(barrier, inc=1, device_id=device, device_id_type=MESH)

    loop(1, n_chip, lambda d: greet(chip_at(d)[1]))
    loop(1, n_ctx, lambda d: greet(ctx_at(d)[1]))
    greet(sibling)
    pl.semaphore_wait(barrier, n_chip + n_ctx - 1)

    for i in range(4):
        use(i)
    lat[c, core, chip, :, :latent] = kv_latent[...]
    gates = gates_ref[...]
    gates_high = gates.astype(BF16).astype(F32)
    tail = jnp.concatenate(
        [
            jnp.zeros((ROPE, rows), F32),
            ids_ref[...].astype(F32),
            gates_high,
            gates - gates_high,
            jnp.zeros((ROPE - 3 * TOPK, rows), F32),
        ],
        axis=0,
    ).T
    lat[c, core, chip, :, latent:] = jnp.concatenate(
        [key_rope[...], tail[:, ROPE:].astype(BF16)], axis=1
    )

    def block_copy(s, d):
        held = (chip + across(s)) % n_chip
        return remote(
            lat.at[s, core, held],
            lat.at[s, core, held],
            lat_ctx_send.at[d],
            lat_ctx_recv.at[s],
            ctx_at(d)[1],
        )

    def half_copy(s, d):
        return remote(
            lat.at[s, core],
            lat.at[s, core],
            lat_ctx_send.at[d],
            lat_ctx_recv.at[s],
            ctx_at(d)[1],
        )

    odd_later = (n_ctx - c) // 2
    even_later = (n_ctx - 1 - c) // 2
    loop(0, odd_later, lambda i: block_copy(c, 2 * i + 1).start())

    def tp_copy(s, d):
        held = (chip + across(s)) % n_chip
        return remote(
            lat.at[s, core, held],
            lat.at[s, core, held],
            lat_tp_send.at[s],
            lat_tp_recv.at[s],
            chip_at(d)[1],
        )

    def tp_all(s):
        blocks = lat.at[s, core, pl.ds(0, n_chip - 1)]
        return remote(blocks, blocks, lat_tp_send.at[s], lat_tp_recv.at[s], sibling)

    loop(1, n_chip, lambda d: tp_copy(c, d).start())

    use(4)
    q_all = queries[...].reshape(n_chip, 2, rows, queries.shape[1])
    for k in range(2):
        q_half = q_all[:, k].reshape(half, queries.shape[1])
        for h in range(heads):
            piece = q_half[:, h * (NOPE + ROPE) : (h + 1) * (NOPE + ROPE)]
            q_s[h, k * half : (k + 1) * half, :] = jnp.concatenate(
                [piece, jnp.zeros((half, 2 * NOPE - NOPE - ROPE), BF16)], axis=1
            )
    top_s[...] = jnp.full(top_s.shape, LOW, F32)
    acc_s[...] = jnp.zeros(acc_s.shape, F32)

    def pass_on(i):
        s = c - 2 * i - 1
        block_copy(s, 1).wait_recv()
        loop(1, n_chip, lambda d: tp_copy(s, d).start())

    loop(0, (c + 1) // 2, pass_on)

    def lat_sent():
        loop(0, odd_later, lambda i: block_copy(c, 2 * i + 1).wait_send())
        loop(0, even_later, lambda i: half_copy(c, 2 * i + 2).wait_send())
        tp_all(c).wait_send()
        loop(0, (c + 1) // 2, lambda i: tp_all(c - 2 * i - 1).wait_send())
        loop(0, c + 1, lambda i: sib_copy(c - i, core).wait_send())

    pending.append(lat_sent)

    scale = (1.0 / math.sqrt(NOPE + ROPE)) * math.log2(math.e)

    def place(index, axis_shape, axis):
        i = lax.broadcasted_iota(jnp.int32, axis_shape, axis) + index
        return ((i & (half - 1)) // rows) * (2 * rows) + (i // half) * rows + (i & (rows - 1))

    def attend(s, k, diagonal):
        block = lat[s, k].reshape(half, lat.shape[4])
        k_s[...] = dot(block[:, :latent], w_key[...]).astype(BF16)
        v_s[...] = dot(block[:, :latent], w_value[...]).astype(BF16)
        rope = block[:, latent:]
        ones = jnp.ones((half, VDIM), BF16)
        for h in range(heads):
            keys = jnp.concatenate([k_s[:, h * NOPE : (h + 1) * NOPE], rope], axis=1)
            values = jnp.concatenate([v_s[:, h * VDIM : (h + 1) * VDIM], ones], axis=1)
            scores = dot_rows(q_s[h], keys)
            if diagonal:
                query_at = place(0, (group, half), 0)
                key_at = place(k * half, (group, half), 1)
                scores = jnp.where(key_at <= query_at, scores, LOW)
            top_old = top_s[h]
            top_new = jnp.maximum(top_old, jnp.max(scores, axis=1, keepdims=True))
            top_s[h] = top_new
            weights = jnp.concatenate(
                [
                    jnp.exp2((scores[:, j * 128 : (j + 1) * 128] - top_new) * scale).astype(BF16)
                    for j in range(half // 128)
                ],
                axis=1,
            )
            factor = jnp.exp2((top_old - top_new) * scale)
            factor = jnp.concatenate([factor, factor], axis=1)
            acc_s[h] = acc_s[h] * factor + dot(weights, values)

    def sib_copy(s, k):
        return remote(lat.at[s, k], lat.at[s, k], lat_sib_send.at[s], lat_sib_recv.at[s], sibling)

    def key_step(i, diagonal):
        s = c - i
        if diagonal:
            tp_all(s).wait_recv()
            loop(0, even_later, lambda i: half_copy(c, 2 * i + 2).start())
        else:

            @pl.when(i % 2 == 1)
            def _():
                tp_all(s).wait_recv()

            @pl.when(i % 2 == 0)
            def _():
                half_copy(s, 2).wait_recv()

        sib_copy(s, core).start()

        def half_step(j):
            @pl.when(j == 1)
            def _():
                sib_copy(s, other).wait_recv()

            attend(s, (core + j) % 2, diagonal)

        loop(0, 2, half_step)

    use(5)
    use(6)
    key_step(0, True)
    loads[9].start()
    loop(1, c + 1, lambda i: key_step(i, False))

    def sib_part(n, buffer, landing, send, recv):
        return remote(
            buffer.at[other, :, :, cols(n)],
            landing.at[:, :, cols(n)],
            send.at[0],
            recv.at[n],
            sibling,
        )

    def row_part(n, d, buffer, landing, send, recv):
        j, device = chip_at(d)
        return remote(
            buffer.at[core, j, :, cols(n)],
            landing.at[chip, :, cols(n)],
            send.at[0],
            recv.at[n],
            device,
        )

    def pass_rows(n, buffer, from_sibling, landing, sib_send, sib_recv, send, recv):
        sib_part(n, buffer, from_sibling, sib_send, sib_recv).wait_recv()
        summed = (
            buffer[core, :, :, cols(n)].astype(F32) + from_sibling[:, :, cols(n)].astype(F32)
        ).astype(BF16)
        buffer[core, :, :, cols(n)] = summed
        landing[chip, :, cols(n)] = buffer[core, chip, :, cols(n)]
        loop(1, n_chip, lambda d: row_part(n, d, buffer, landing, send, recv).start())

    def rows_sent(buffer, from_sibling, landing, sib_send, sib_recv, send, recv):
        remote(
            buffer.at[other], from_sibling, sib_send.at[0], sib_recv.at[0], sibling
        ).wait_send()
        others = pl.ds(0, n_chip - 1)
        remote(
            buffer.at[core, others], landing.at[others], send.at[0], recv.at[0], sibling
        ).wait_send()

    def sum_rows(n, landing, send, recv):
        blocks = landing.at[pl.ds(0, n_chip - 1), :, cols(n)]
        remote(blocks, blocks, send.at[0], recv.at[n], sibling).wait_recv()
        return jnp.sum(landing[:, :, cols(n)].astype(F32), axis=0)

    attention = jnp.concatenate(
        [(acc_s[h, :, :VDIM] / acc_s[h, :, VDIM:]).astype(BF16) for h in range(heads)], axis=1
    )
    use(9)
    first = (part, sib_in, row_in, a_sib_send, a_sib_recv, a_row_send, a_row_recv)
    for n in range(CHUNKS):
        part[:, :, :, cols(n)] = (
            dot(attention, w_out[:, cols(n)]).astype(BF16).reshape(2, n_chip, rows, span)
        )
        sib_part(n, part, sib_in, a_sib_send, a_sib_recv).start()
        if n > 0:
            pass_rows(n - 1, *first)
    pass_rows(CHUNKS - 1, *first)
    pending.append(functools.partial(rows_sent, *first))

    for load in loads[10:]:
        load.start()

    meta = lat[c, :, :, :, latent:].reshape(group, lat.shape[4] - latent).astype(F32).T
    ids = meta[ROPE : ROPE + TOPK]
    gates_all = meta[ROPE + TOPK : ROPE + 2 * TOPK] + meta[ROPE + 2 * TOPK : ROPE + 3 * TOPK]
    expert_row = lax.broadcasted_iota(jnp.int32, (16, group), 0)
    owner = expert_row * (2 * n_chip) + ((chip + across(expert_row)) % n_chip) * 2 + core
    expert = jnp.where(expert_row < n_ctx, owner, -1).astype(F32)
    member = jnp.zeros((16, group), F32)
    gate = jnp.zeros((16, group), F32)
    for k in range(TOPK):
        same = ids[k : k + 1] == expert
        member = member + jnp.where(same, 1.0, 0.0)
        gate = gate + jnp.where(same, gates_all[k : k + 1], 0.0)
    before = lax.broadcasted_iota(jnp.int32, (group, group), 0) < lax.broadcasted_iota(
        jnp.int32, (group, group), 1
    )
    rank = dot(member.astype(BF16), jnp.where(before, 1.0, 0.0).astype(BF16))
    slot = lax.broadcasted_iota(jnp.int32, (slot_room, group), 0).astype(F32)
    for e in range(n_ctx):
        chosen = jnp.where(member[e : e + 1] > 0.5, rank[e : e + 1], -1.0) == slot
        pick[e] = jnp.where(chosen, 1.0, 0.0).astype(BF16)
        give[e] = jnp.where(chosen, gate[e : e + 1], 0.0).astype(BF16)

    use(7)
    use(8)
    for n in range(CHUNKS):
        hidden[:, cols(n)] = residual[:, cols(n)].astype(F32) + sum_rows(
            n, row_in, a_row_send, a_row_recv
        )
    state = hidden[...]
    mean_square = jnp.mean(state * state, axis=1, keepdims=True)
    normed[core, chip] = (state * lax.rsqrt(mean_square + 1e-06) * gain[...].reshape(1, width)).astype(BF16)

    def normed_copy(n, d):
        block = normed.at[core, chip, :, cols(n)]
        return remote(block, block, n_send.at[0], n_recv.at[n], chip_at(d)[1])

    def normed_all(n):
        blocks = normed.at[core, pl.ds(0, n_chip - 1), :, cols(n)]
        return remote(blocks, blocks, n_send.at[0], n_recv.at[n], sibling)

    def normed_sib(n):
        half_rows = normed.at[core, :, :, cols(n)]
        return remote(half_rows, half_rows, n_sib_send.at[0], n_sib_recv.at[n], sibling)

    def normed_sent():
        blocks = normed.at[core, pl.ds(0, n_chip - 1)]
        remote(blocks, blocks, n_send.at[0], n_recv.at[0], sibling).wait_send()
        half_rows = normed.at[core]
        remote(half_rows, half_rows, n_sib_send.at[0], n_sib_recv.at[0], sibling).wait_send()

    for n in range(CHUNKS):
        loop(1, n_chip, lambda d: normed_copy(n, d).start())
    pending.append(normed_sent)

    def slot_copy(n, d, source, landing, send, recv):
        j, device = ctx_at(d)
        return remote(
            source.at[j, :, cols(n)], landing.at[c, :, cols(n)], send.at[0], recv.at[n], device
        )

    def slot_wait(n, source, landing, send, recv):
        blocks = landing.at[pl.ds(0, n_ctx - 1), :, cols(n)]
        remote(blocks, blocks, send.at[0], recv.at[n], sibling).wait_recv()

    def slots_sent(source, landing, send, recv):
        blocks = source.at[pl.ds(0, n_ctx - 1)]
        remote(blocks, blocks, send.at[0], recv.at[0], sibling).wait_send()

    there = (slots_out, slots_in, x_send, x_recv)
    back = (back_out, back_in, y_send, y_recv)
    for n in range(CHUNKS):
        normed_all(n).wait_recv()
        normed_sib(n).start()
        normed_sib(n).wait_recv()
        block = normed[:, :, :, cols(n)].reshape(group, span)
        picked = dot(pick[...].reshape(n_ctx * slot_room, group), block).astype(BF16)
        slots_out[:, :, cols(n)] = picked.reshape(n_ctx, slot_room, span)
        loop(1, n_ctx, lambda d: slot_copy(n, d, *there).start())
        slots_in[c, :, cols(n)] = slots_out[c, :, cols(n)]
    pending.append(functools.partial(slots_sent, *there))

    use(10)
    use(11)
    everyone = normed[...].reshape(group, width)
    gate_part = dot_rows(everyone, shared_gate[...])
    up_part = dot_rows(everyone, shared_up[...])
    shared_hidden = (gate_part / (1.0 + jnp.exp(-gate_part)) * up_part).astype(BF16)
    use(12)
    for n in range(CHUNKS):
        shared_acc[:, cols(n)] = dot(shared_hidden, shared_down[:, cols(n)])

    use(13)
    use(14)
    for n in range(CHUNKS):
        slot_wait(n, *there)
        items = slots_in[:, :, cols(n)].reshape(n_ctx * slot_room, span)
        product = dot(items, gate_up[cols(n), :])
        if n == 0:
            up_acc[...] = product
        else:
            up_acc[...] = up_acc[...] + product
    inner = down.shape[0]
    gate_part = up_acc[:, :inner]
    expert_hidden = (gate_part / (1.0 + jnp.exp(-gate_part)) * up_acc[:, inner:]).astype(BF16)
    for n in range(CHUNKS):
        result = dot(expert_hidden, down[:, cols(n)]).astype(BF16)
        back_out[:, :, cols(n)] = result.reshape(n_ctx, slot_room, span)
        loop(1, n_ctx, lambda d: slot_copy(n, d, *back).start())
        back_in[c, :, cols(n)] = back_out[c, :, cols(n)]
    pending.append(functools.partial(slots_sent, *back))

    give_rows = give[...].reshape(n_ctx * slot_room, group).astype(F32).T.astype(BF16)
    second = (part2, sib_in2, row_in2, b_sib_send, b_sib_recv, b_row_send, b_row_recv)
    for n in range(CHUNKS):
        slot_wait(n, *back)
        returned = back_in[:, :, cols(n)].reshape(n_ctx * slot_room, span)
        both = shared_acc[:, cols(n)] + dot(give_rows, returned)
        part2[:, :, :, cols(n)] = both.astype(BF16).reshape(2, n_chip, rows, span)
        sib_part(n, part2, sib_in2, b_sib_send, b_sib_recv).start()
        if n > 0:
            pass_rows(n - 1, *second)
    pass_rows(CHUNKS - 1, *second)
    pending.append(functools.partial(rows_sent, *second))
    for n in range(CHUNKS):
        out_ref[:, cols(n)] = (
            hidden[:, cols(n)] + sum_rows(n, row_in2, b_row_send, b_row_recv)
        ).astype(BF16)

    finish()


def shards(
    n_ctx,
    n_tp,
    queries,
    kv_latent,
    key_rope,
    w_key,
    w_value,
    w_out,
    residual,
    moe_gain,
    shared_gate,
    shared_up,
    shared_down,
    expert_gate_up,
    expert_down,
    expert_ids,
    gate_weights,
):
    rows, width = residual.shape
    n_chip = n_tp // 2
    heads = w_key.shape[1] // NOPE
    group = rows * n_tp
    latent = kv_latent.shape[1]
    slot_room = CAP * n_tp
    dma = pltpu.SemaphoreType.DMA
    scratch = [
        pltpu.VMEM(kv_latent.shape, BF16),
        pltpu.VMEM(key_rope.shape, BF16),
        pltpu.VMEM(expert_ids.shape[::-1], jnp.int32),
        pltpu.VMEM(gate_weights.shape[::-1], F32),
        pltpu.VMEM(queries.shape, BF16),
        pltpu.VMEM(w_key.shape, BF16),
        pltpu.VMEM(w_value.shape, BF16),
        pltpu.VMEM(residual.shape, BF16),
        pltpu.VMEM(moe_gain.shape, F32),
        pltpu.VMEM(w_out.shape, BF16),
        pltpu.VMEM(shared_gate.shape[::-1], BF16),
        pltpu.VMEM(shared_up.shape[::-1], BF16),
        pltpu.VMEM(shared_down.shape, BF16),
        pltpu.VMEM(expert_gate_up.shape[1:], BF16),
        pltpu.VMEM(expert_down.shape[1:], BF16),
        dma((15,)),
        pltpu.VMEM((n_ctx, 2, n_chip, rows, latent + 128), BF16),
        pltpu.VMEM((heads, group, 2 * NOPE), BF16),
        pltpu.VMEM((group // 2, heads * NOPE), BF16),
        pltpu.VMEM((group // 2, heads * VDIM), BF16),
        pltpu.VMEM((heads, group, 128), F32),
        pltpu.VMEM((heads, group, 2 * VDIM), F32),
        dma((n_ctx,)),
        dma((n_ctx,)),
        dma((n_ctx,)),
        dma((n_ctx,)),
        dma((n_ctx,)),
        dma((n_ctx,)),
        pltpu.VMEM((2, n_chip, rows, width), BF16),
        pltpu.VMEM((n_chip, rows, width), BF16),
        pltpu.VMEM((n_chip, rows, width), BF16),
        dma((1,)),
        dma((CHUNKS,)),
        dma((1,)),
        dma((CHUNKS,)),
        pltpu.VMEM((rows, width), F32),
        pltpu.VMEM((2, n_chip, rows, width), BF16),
        dma((1,)),
        dma((CHUNKS,)),
        dma((1,)),
        dma((CHUNKS,)),
        pltpu.VMEM((n_ctx, slot_room, group), BF16),
        pltpu.VMEM((n_ctx, slot_room, group), BF16),
        pltpu.VMEM((n_ctx, slot_room, width), BF16),
        pltpu.VMEM((n_ctx, slot_room, width), BF16),
        pltpu.VMEM((n_ctx * slot_room, expert_gate_up.shape[2]), F32),
        dma((1,)),
        dma((CHUNKS,)),
        pltpu.VMEM((n_ctx, slot_room, width), BF16),
        pltpu.VMEM((n_ctx, slot_room, width), BF16),
        dma((1,)),
        dma((CHUNKS,)),
        pltpu.VMEM((group, width), F32),
        pltpu.VMEM((2, n_chip, rows, width), BF16),
        pltpu.VMEM((n_chip, rows, width), BF16),
        pltpu.VMEM((n_chip, rows, width), BF16),
        dma((1,)),
        dma((CHUNKS,)),
        dma((1,)),
        dma((CHUNKS,)),
    ]
    vmem = pl.BlockSpec(memory_space=pltpu.VMEM)
    hbm = pl.BlockSpec(memory_space=pl.ANY)
    return pl.pallas_call(
        layer_kernel,
        out_shape=jax.ShapeDtypeStruct((rows, width), BF16),
        in_specs=[hbm] * 15,
        out_specs=vmem,
        scratch_shapes=scratch,
        compiler_params=pltpu.CompilerParams(
            collective_id=1, has_side_effects=True, vmem_limit_bytes=63 * 1024 * 1024
        ),
        cost_estimate=pl.CostEstimate(
            flops=20_000_000_000, bytes_accessed=20_000_000, transcendentals=9_000_000
        ),
        name="layer",
    )(
        queries,
        kv_latent,
        key_rope,
        w_key,
        w_value,
        w_out,
        residual,
        moe_gain,
        shared_gate.T,
        shared_up.T,
        shared_down,
        expert_gate_up,
        expert_down,
        expert_ids.T,
        gate_weights.T,
    )


def solution(mesh):
    in_specs = (
        P("ctx", "tp"),
        P(("ctx", "tp"), None),
        P(("ctx", "tp"), None),
        P(None, "tp"),
        P(None, "tp"),
        P("tp", None),
        P(("ctx", "tp"), None),
        P(),
        P(None, "tp"),
        P(None, "tp"),
        P("tp", None),
        P(("ctx", "tp"), None, None),
        P(("ctx", "tp"), None, None),
        P(("ctx", "tp"), None),
        P(("ctx", "tp"), None),
    )
    out_specs = P(("ctx", "tp"), None)
    return jax.shard_map(
        functools.partial(shards, mesh.shape["ctx"], mesh.shape["tp"]),
        mesh=mesh,
        in_specs=in_specs,
        out_specs=out_specs,
        check_vma=False,
    )
```

```python
import functools
import math

import jax
import jax.numpy as jnp
from jax import lax
from jax.experimental import pallas as pl
from jax.experimental.pallas import tpu as pltpu
from jax.sharding import PartitionSpec as P

NOPE = 128
ROPE = 64
VDIM = 128
TOPK = 6
CAP = 3
MESH = pl.DeviceIdType.MESH
F32 = jnp.float32
BF16 = jnp.bfloat16
LOW = -1e30
CHUNKS = 10
LEAD = 3


def loop(first, end, body):
    if isinstance(first, int) and isinstance(end, int):
        for i in range(first, end):
            body(i)
        return

    def step(i, carry):
        body(i)
        return carry

    lax.fori_loop(first, end, step, 0)


def dot(a, b):
    return jnp.dot(a, b, preferred_element_type=F32)


def dot_rows(a, b):
    return lax.dot_general(a, b, (((1,), (1,)), ((), ())), preferred_element_type=F32)


def layer_kernel(
    queries_hbm,
    kv_latent_hbm,
    key_rope_hbm,
    w_key_hbm,
    w_value_hbm,
    w_out_hbm,
    residual_hbm,
    gain_hbm,
    shared_gate_hbm,
    shared_up_hbm,
    shared_down_hbm,
    gate_up_hbm,
    down_hbm,
    ids_hbm,
    gates_hbm,
    out_ref,
    kv_latent,
    key_rope,
    ids_ref,
    gates_ref,
    queries,
    w_key,
    w_value,
    residual,
    gain,
    w_out,
    shared_gate,
    shared_up,
    shared_down,
    gate_up,
    down,
    load_sem,
    lat,
    q_s,
    k_s,
    v_s,
    top_s,
    acc_s,
    lat_ctx_send,
    lat_ctx_recv,
    lat_tp_send,
    lat_tp_recv,
    lat_sib_send,
    lat_sib_recv,
    part,
    sib_in,
    row_in,
    a_sib_send,
    a_sib_recv,
    a_row_send,
    a_row_recv,
    hidden,
    normed,
    n_send,
    n_recv,
    n_sib_send,
    n_sib_recv,
    pick,
    give,
    slots_out,
    slots_in,
    up_acc,
    x_send,
    x_recv,
    back_out,
    back_in,
    y_send,
    y_recv,
    shared_acc,
    part2,
    sib_in2,
    row_in2,
    b_sib_send,
    b_sib_recv,
    b_row_send,
    b_row_recv,
):
    c = lax.axis_index("ctx")
    t = lax.axis_index("tp")
    chip = t // 2
    core = t % 2
    other = 1 - core
    sibling = (c, chip * 2 + other)
    rows = residual.shape[0]
    width = residual.shape[1]
    heads = q_s.shape[0]
    latent = w_key.shape[0]
    n_ctx, _, n_chip = lat.shape[:3]
    half = n_chip * rows
    group = 2 * half
    span = width // CHUNKS
    slot_room = slots_out.shape[1]

    def cols(n):
        return pl.ds(n * span, span)

    def remote(src, dst, send, recv, device):
        return pltpu.make_async_remote_copy(
            src_ref=src,
            dst_ref=dst,
            send_sem=send,
            recv_sem=recv,
            device_id=device,
            device_id_type=MESH,
        )

    def chip_at(d):
        j = (chip + d) % n_chip
        return j, (c, j * 2 + core)

    def across(j):
        return ((j + c) % 2) * (n_chip // 2)

    def ctx_at(d):
        j = (c + d) % n_ctx
        return j, (j, ((chip + across(j)) % n_chip) * 2 + core)

    loads = []
    for i, (src, dst) in enumerate(
        (
            (kv_latent_hbm, kv_latent),
            (key_rope_hbm, key_rope),
            (ids_hbm, ids_ref),
            (gates_hbm, gates_ref),
            (queries_hbm, queries),
            (w_key_hbm, w_key),
            (w_value_hbm, w_value),
            (residual_hbm, residual),
            (gain_hbm, gain),
            (w_out_hbm, w_out),
            (shared_gate_hbm, shared_gate),
            (shared_up_hbm, shared_up),
            (shared_down_hbm, shared_down),
            (gate_up_hbm.at[0], gate_up),
            (down_hbm.at[0], down),
        )
    ):
        load = pltpu.make_async_copy(src, dst, load_sem.at[i])
        loads.append(load)
    for load in loads[:9]:
        load.start()
    loaded = set()

    def use(i):
        loaded.add(i)
        loads[i].wait()

    pending = []

    def finish():
        for i in range(len(loads)):
            if i not in loaded and (i < 9 or len(pending) > 1 or (pending and i < 10)):
                use(i)
        for wait in pending:
            wait()

    barrier = pltpu.get_barrier_semaphore()

    def greet(device):
        pl.semaphore_signal(barrier, inc=1, device_id=device, device_id_type=MESH)

    loop(1, n_chip, lambda d: greet(chip_at(d)[1]))
    loop(1, n_ctx, lambda d: greet(ctx_at(d)[1]))
    greet(sibling)
    pl.semaphore_wait(barrier, n_chip + n_ctx - 1)

    for i in range(4):
        use(i)
    lat[c, core, chip, :, :latent] = kv_latent[...]
    gates = gates_ref[...]
    gates_high = gates.astype(BF16).astype(F32)
    tail = jnp.concatenate(
        [
            jnp.zeros((ROPE, rows), F32),
            ids_ref[...].astype(F32),
            gates_high,
            gates - gates_high,
            jnp.zeros((ROPE - 3 * TOPK, rows), F32),
        ],
        axis=0,
    ).T
    lat[c, core, chip, :, latent:] = jnp.concatenate(
        [key_rope[...], tail[:, ROPE:].astype(BF16)], axis=1
    )

    def block_copy(s, d):
        held = (chip + across(s)) % n_chip
        return remote(
            lat.at[s, core, held],
            lat.at[s, core, held],
            lat_ctx_send.at[d],
            lat_ctx_recv.at[s],
            ctx_at(d)[1],
        )

    def half_copy(s, d):
        return remote(
            lat.at[s, core],
            lat.at[s, core],
            lat_ctx_send.at[d],
            lat_ctx_recv.at[s],
            ctx_at(d)[1],
        )

    odd = c % 2
    later = (n_ctx - 1 - c) // 2
    earlier = c // 2
    loop(0, later, lambda i: block_copy(c, 2 * (later - i) + 1 - 2 * odd).start())

    def tp_copy(s, d):
        held = (chip + across(s)) % n_chip
        return remote(
            lat.at[s, core, held],
            lat.at[s, core, held],
            lat_tp_send.at[s],
            lat_tp_recv.at[s],
            chip_at(d)[1],
        )

    def tp_all(s):
        blocks = lat.at[s, core, pl.ds(0, n_chip - 1)]
        return remote(blocks, blocks, lat_tp_send.at[s], lat_tp_recv.at[s], sibling)

    loop(1, n_chip, lambda d: tp_copy(c, d).start())

    use(4)
    q_all = queries[...].reshape(n_chip, 2, rows, queries.shape[1])
    for k in range(2):
        q_half = q_all[:, k].reshape(half, queries.shape[1])
        for h in range(heads):
            piece = q_half[:, h * (NOPE + ROPE) : (h + 1) * (NOPE + ROPE)]
            q_s[h, k * half : (k + 1) * half, :] = jnp.concatenate(
                [piece, jnp.zeros((half, 2 * NOPE - NOPE - ROPE), BF16)], axis=1
            )
    top_s[...] = jnp.full(top_s.shape, LOW, F32)
    acc_s[...] = jnp.zeros(acc_s.shape, F32)

    def pass_on(i):
        s = c - 2 * i - 1 - 2 * odd
        block_copy(s, 1).wait_recv()
        loop(1, n_chip, lambda d: tp_copy(s, d).start())

    loop(0, earlier, pass_on)

    def lat_sent():
        loop(0, later, lambda i: block_copy(c, 2 * (later - i) + 1 - 2 * odd).wait_send())
        loop(0, later, lambda i: half_copy(c, 2 * (later - i)).wait_send())

        @pl.when(odd == 0)
        def _():
            half_copy(c, 1).wait_send()

        tp_all(c).wait_send()
        loop(0, earlier, lambda i: tp_all(c - 2 * i - 1 - 2 * odd).wait_send())
        loop(0, c + 1, lambda i: sib_copy(c - i, core).wait_send())

    pending.append(lat_sent)

    scale = (1.0 / math.sqrt(NOPE + ROPE)) * math.log2(math.e)

    def place(index, axis_shape, axis):
        i = lax.broadcasted_iota(jnp.int32, axis_shape, axis) + index
        return ((i & (half - 1)) // rows) * (2 * rows) + (i // half) * rows + (i & (rows - 1))

    def attend(s, k, diagonal):
        block = lat[s, k].reshape(half, lat.shape[4])
        k_s[...] = dot(block[:, :latent], w_key[...]).astype(BF16)
        v_s[...] = dot(block[:, :latent], w_value[...]).astype(BF16)
        rope = block[:, latent:]
        ones = jnp.ones((half, VDIM), BF16)
        for h in range(heads):
            keys = jnp.concatenate([k_s[:, h * NOPE : (h + 1) * NOPE], rope], axis=1)
            values = jnp.concatenate([v_s[:, h * VDIM : (h + 1) * VDIM], ones], axis=1)
            scores = dot_rows(q_s[h], keys)
            if diagonal:
                query_at = place(0, (group, half), 0)
                key_at = place(k * half, (group, half), 1)
                scores = jnp.where(key_at <= query_at, scores, LOW)
            top_old = top_s[h]
            top_new = jnp.maximum(top_old, jnp.max(scores, axis=1, keepdims=True))
            top_s[h] = top_new
            weights = jnp.concatenate(
                [
                    jnp.exp2((scores[:, j * 128 : (j + 1) * 128] - top_new) * scale).astype(BF16)
                    for j in range(half // 128)
                ],
                axis=1,
            )
            factor = jnp.exp2((top_old - top_new) * scale)
            factor = jnp.concatenate([factor, factor], axis=1)
            acc_s[h] = acc_s[h] * factor + dot(weights, values)

    def sib_copy(s, k):
        return remote(lat.at[s, k], lat.at[s, k], lat_sib_send.at[s], lat_sib_recv.at[s], sibling)

    def key_step(q, diagonal):
        if diagonal:
            s = c
            tp_all(s).wait_recv()

            @pl.when(odd == 0)
            def _():
                half_copy(c, 1).start()

            loop(0, later, lambda i: half_copy(c, 2 * (later - i)).start())
        else:
            whole = q // (earlier + 1)
            r = jnp.maximum(q - earlier, 1)
            across_whole = odd * (1 // r)
            back = (1 - whole) * (2 * q - 1 + 2 * odd) + whole * (2 * (r - odd) + across_whole)
            s = c - back

            @pl.when(whole == 0)
            def _():
                tp_all(s).wait_recv()

            @pl.when(whole == 1)
            def _():
                half_copy(s, 2).wait_recv()

        sib_copy(s, core).start()

        def half_step(j):
            @pl.when(j == 1)
            def _():
                sib_copy(s, other).wait_recv()

            attend(s, (core + j) % 2, diagonal)

        loop(0, 2, half_step)

    use(5)
    use(6)
    key_step(0, True)
    loads[9].start()
    loop(1, c + 1, lambda i: key_step(i, False))

    def sib_part(n, buffer, landing, send, recv):
        return remote(
            buffer.at[other, :, :, cols(n)],
            landing.at[:, :, cols(n)],
            send.at[0],
            recv.at[n],
            sibling,
        )

    def row_part(n, d, buffer, landing, send, recv):
        j, device = chip_at(d)
        return remote(
            buffer.at[core, j, :, cols(n)],
            landing.at[chip, :, cols(n)],
            send.at[0],
            recv.at[n],
            device,
        )

    def pass_rows(n, buffer, from_sibling, landing, sib_send, sib_recv, send, recv):
        sib_part(n, buffer, from_sibling, sib_send, sib_recv).wait_recv()
        summed = (
            buffer[core, :, :, cols(n)].astype(F32) + from_sibling[:, :, cols(n)].astype(F32)
        ).astype(BF16)
        buffer[core, :, :, cols(n)] = summed
        landing[chip, :, cols(n)] = buffer[core, chip, :, cols(n)]
        loop(1, n_chip, lambda d: row_part(n, d, buffer, landing, send, recv).start())

    def rows_sent(buffer, from_sibling, landing, sib_send, sib_recv, send, recv):
        remote(
            buffer.at[other], from_sibling, sib_send.at[0], sib_recv.at[0], sibling
        ).wait_send()
        others = pl.ds(0, n_chip - 1)
        remote(
            buffer.at[core, others], landing.at[others], send.at[0], recv.at[0], sibling
        ).wait_send()

    def sum_rows(n, landing, send, recv):
        blocks = landing.at[pl.ds(0, n_chip - 1), :, cols(n)]
        remote(blocks, blocks, send.at[0], recv.at[n], sibling).wait_recv()
        return jnp.sum(landing[:, :, cols(n)].astype(F32), axis=0)

    attention = jnp.concatenate(
        [(acc_s[h, :, :VDIM] / acc_s[h, :, VDIM:]).astype(BF16) for h in range(heads)], axis=1
    )
    use(9)
    first = (part, sib_in, row_in, a_sib_send, a_sib_recv, a_row_send, a_row_recv)
    for n in range(CHUNKS):
        part[:, :, :, cols(n)] = (
            dot(attention, w_out[:, cols(n)]).astype(BF16).reshape(2, n_chip, rows, span)
        )
        sib_part(n, part, sib_in, a_sib_send, a_sib_recv).start()
        if n > 0:
            pass_rows(n - 1, *first)
    pass_rows(CHUNKS - 1, *first)
    pending.append(functools.partial(rows_sent, *first))

    for load in loads[10:]:
        load.start()

    meta = lat[c, :, :, :, latent:].reshape(group, lat.shape[4] - latent).astype(F32).T
    ids = meta[ROPE : ROPE + TOPK]
    gates_all = meta[ROPE + TOPK : ROPE + 2 * TOPK] + meta[ROPE + 2 * TOPK : ROPE + 3 * TOPK]
    expert_row = lax.broadcasted_iota(jnp.int32, (16, group), 0)
    owner = expert_row * (2 * n_chip) + ((chip + across(expert_row)) % n_chip) * 2 + core
    expert = jnp.where(expert_row < n_ctx, owner, -1).astype(F32)
    member = jnp.zeros((16, group), F32)
    gate = jnp.zeros((16, group), F32)
    for k in range(TOPK):
        same = ids[k : k + 1] == expert
        member = member + jnp.where(same, 1.0, 0.0)
        gate = gate + jnp.where(same, gates_all[k : k + 1], 0.0)
    before = lax.broadcasted_iota(jnp.int32, (group, group), 0) < lax.broadcasted_iota(
        jnp.int32, (group, group), 1
    )
    rank = dot(member.astype(BF16), jnp.where(before, 1.0, 0.0).astype(BF16))
    slot = lax.broadcasted_iota(jnp.int32, (slot_room, group), 0).astype(F32)
    for e in range(n_ctx):
        chosen = jnp.where(member[e : e + 1] > 0.5, rank[e : e + 1], -1.0) == slot
        pick[e] = jnp.where(chosen, 1.0, 0.0).astype(BF16)
        give[e] = jnp.where(chosen, gate[e : e + 1], 0.0).astype(BF16)

    def normed_copy(n, d):
        block = normed.at[core, chip, :, cols(n)]
        return remote(block, block, n_send.at[0], n_recv.at[n], chip_at(d)[1])

    def normed_all(n):
        blocks = normed.at[core, pl.ds(0, n_chip - 1), :, cols(n)]
        return remote(blocks, blocks, n_send.at[0], n_recv.at[n], sibling)

    def normed_sib(n):
        half_rows = normed.at[core, :, :, cols(n)]
        return remote(half_rows, half_rows, n_sib_send.at[0], n_sib_recv.at[n], sibling)

    def normed_sent():
        blocks = normed.at[core, pl.ds(0, n_chip - 1)]
        remote(blocks, blocks, n_send.at[0], n_recv.at[0], sibling).wait_send()
        half_rows = normed.at[core]
        remote(half_rows, half_rows, n_sib_send.at[0], n_sib_recv.at[0], sibling).wait_send()

    def send_rows(n):
        state = residual[:, cols(n)].astype(F32) + sum_rows(n, row_in, a_row_send, a_row_recv)
        hidden[:, cols(n)] = state
        normed[core, chip, :, cols(n)] = (state * gain[cols(n)].reshape(1, span)).astype(BF16)
        loop(1, n_chip, lambda d: normed_copy(n, d).start())

    def square_sum(block, n):
        plain = block.astype(F32) * (1.0 / gain[cols(n)].reshape(1, span))
        return jnp.sum(plain * plain, axis=1, keepdims=True)

    def norm_factor(total):
        return lax.rsqrt(total * (1.0 / width) + 1e-06)

    use(7)
    use(8)
    for n in range(LEAD):
        send_rows(n)
    pending.append(normed_sent)

    def slot_copy(n, d, source, landing, send, recv):
        j, device = ctx_at(d)
        return remote(
            source.at[j, :, cols(n)], landing.at[c, :, cols(n)], send.at[0], recv.at[n], device
        )

    def slot_wait(n, source, landing, send, recv):
        blocks = landing.at[pl.ds(0, n_ctx - 1), :, cols(n)]
        remote(blocks, blocks, send.at[0], recv.at[n], sibling).wait_recv()

    def slots_sent(source, landing, send, recv):
        blocks = source.at[pl.ds(0, n_ctx - 1)]
        remote(blocks, blocks, send.at[0], recv.at[0], sibling).wait_send()

    there = (slots_out, slots_in, x_send, x_recv)
    back = (back_out, back_in, y_send, y_recv)
    group_squares = 0.0
    for n in range(CHUNKS):
        if n + LEAD < CHUNKS:
            send_rows(n + LEAD)
        normed_all(n).wait_recv()
        normed_sib(n).start()
        normed_sib(n).wait_recv()
        block = normed[:, :, :, cols(n)].reshape(group, span)
        picked = dot(pick[...].reshape(n_ctx * slot_room, group), block).astype(BF16)
        slots_out[:, :, cols(n)] = picked.reshape(n_ctx, slot_room, span)
        loop(1, n_ctx, lambda d: slot_copy(n, d, *there).start())
        slots_in[c, :, cols(n)] = slots_out[c, :, cols(n)]
        group_squares = group_squares + square_sum(block, n)
    pending.append(functools.partial(slots_sent, *there))

    use(10)
    use(11)
    everyone = normed[...].reshape(group, width)
    factor = norm_factor(group_squares)
    gate_part = dot_rows(everyone, shared_gate[...]) * factor
    up_part = dot_rows(everyone, shared_up[...]) * factor
    shared_hidden = (gate_part / (1.0 + jnp.exp(-gate_part)) * up_part).astype(BF16)
    use(12)
    for n in range(CHUNKS):
        shared_acc[:, cols(n)] = dot(shared_hidden, shared_down[:, cols(n)])

    use(13)
    use(14)
    slot_squares = 0.0
    for n in range(CHUNKS):
        slot_wait(n, *there)
        items = slots_in[:, :, cols(n)].reshape(n_ctx * slot_room, span)
        product = dot(items, gate_up[cols(n), :])
        slot_squares = slot_squares + square_sum(items, n)
        if n == 0:
            up_acc[...] = product
        else:
            up_acc[...] = up_acc[...] + product
    inner = down.shape[0]
    factor = norm_factor(slot_squares)
    gate_part = up_acc[:, :inner] * factor
    up_part = up_acc[:, inner:] * factor
    expert_hidden = (gate_part / (1.0 + jnp.exp(-gate_part)) * up_part).astype(BF16)
    for n in range(CHUNKS):
        result = dot(expert_hidden, down[:, cols(n)]).astype(BF16)
        back_out[:, :, cols(n)] = result.reshape(n_ctx, slot_room, span)
        loop(1, n_ctx, lambda d: slot_copy(n, d, *back).start())
        back_in[c, :, cols(n)] = back_out[c, :, cols(n)]
    pending.append(functools.partial(slots_sent, *back))

    give_rows = give[...].reshape(n_ctx * slot_room, group).astype(F32).T.astype(BF16)
    second = (part2, sib_in2, row_in2, b_sib_send, b_sib_recv, b_row_send, b_row_recv)
    for n in range(CHUNKS):
        slot_wait(n, *back)
        returned = back_in[:, :, cols(n)].reshape(n_ctx * slot_room, span)
        both = shared_acc[:, cols(n)] + dot(give_rows, returned)
        part2[:, :, :, cols(n)] = both.astype(BF16).reshape(2, n_chip, rows, span)
        sib_part(n, part2, sib_in2, b_sib_send, b_sib_recv).start()
        if n > 0:
            pass_rows(n - 1, *second)
    pass_rows(CHUNKS - 1, *second)
    pending.append(functools.partial(rows_sent, *second))
    for n in range(CHUNKS):
        out_ref[:, cols(n)] = (
            hidden[:, cols(n)] + sum_rows(n, row_in2, b_row_send, b_row_recv)
        ).astype(BF16)

    finish()


def shards(
    n_ctx,
    n_tp,
    queries,
    kv_latent,
    key_rope,
    w_key,
    w_value,
    w_out,
    residual,
    moe_gain,
    shared_gate,
    shared_up,
    shared_down,
    expert_gate_up,
    expert_down,
    expert_ids,
    gate_weights,
):
    rows, width = residual.shape
    n_chip = n_tp // 2
    heads = w_key.shape[1] // NOPE
    group = rows * n_tp
    latent = kv_latent.shape[1]
    slot_room = CAP * n_tp
    dma = pltpu.SemaphoreType.DMA
    scratch = [
        pltpu.VMEM(kv_latent.shape, BF16),
        pltpu.VMEM(key_rope.shape, BF16),
        pltpu.VMEM(expert_ids.shape[::-1], jnp.int32),
        pltpu.VMEM(gate_weights.shape[::-1], F32),
        pltpu.VMEM(queries.shape, BF16),
        pltpu.VMEM(w_key.shape, BF16),
        pltpu.VMEM(w_value.shape, BF16),
        pltpu.VMEM(residual.shape, BF16),
        pltpu.VMEM(moe_gain.shape, F32),
        pltpu.VMEM(w_out.shape, BF16),
        pltpu.VMEM(shared_gate.shape[::-1], BF16),
        pltpu.VMEM(shared_up.shape[::-1], BF16),
        pltpu.VMEM(shared_down.shape, BF16),
        pltpu.VMEM(expert_gate_up.shape[1:], BF16),
        pltpu.VMEM(expert_down.shape[1:], BF16),
        dma((15,)),
        pltpu.VMEM((n_ctx, 2, n_chip, rows, latent + 128), BF16),
        pltpu.VMEM((heads, group, 2 * NOPE), BF16),
        pltpu.VMEM((group // 2, heads * NOPE), BF16),
        pltpu.VMEM((group // 2, heads * VDIM), BF16),
        pltpu.VMEM((heads, group, 128), F32),
        pltpu.VMEM((heads, group, 2 * VDIM), F32),
        dma((n_ctx,)),
        dma((n_ctx,)),
        dma((n_ctx,)),
        dma((n_ctx,)),
        dma((n_ctx,)),
        dma((n_ctx,)),
        pltpu.VMEM((2, n_chip, rows, width), BF16),
        pltpu.VMEM((n_chip, rows, width), BF16),
        pltpu.VMEM((n_chip, rows, width), BF16),
        dma((1,)),
        dma((CHUNKS,)),
        dma((1,)),
        dma((CHUNKS,)),
        pltpu.VMEM((rows, width), F32),
        pltpu.VMEM((2, n_chip, rows, width), BF16),
        dma((1,)),
        dma((CHUNKS,)),
        dma((1,)),
        dma((CHUNKS,)),
        pltpu.VMEM((n_ctx, slot_room, group), BF16),
        pltpu.VMEM((n_ctx, slot_room, group), BF16),
        pltpu.VMEM((n_ctx, slot_room, width), BF16),
        pltpu.VMEM((n_ctx, slot_room, width), BF16),
        pltpu.VMEM((n_ctx * slot_room, expert_gate_up.shape[2]), F32),
        dma((1,)),
        dma((CHUNKS,)),
        pltpu.VMEM((n_ctx, slot_room, width), BF16),
        pltpu.VMEM((n_ctx, slot_room, width), BF16),
        dma((1,)),
        dma((CHUNKS,)),
        pltpu.VMEM((group, width), F32),
        pltpu.VMEM((2, n_chip, rows, width), BF16),
        pltpu.VMEM((n_chip, rows, width), BF16),
        pltpu.VMEM((n_chip, rows, width), BF16),
        dma((1,)),
        dma((CHUNKS,)),
        dma((1,)),
        dma((CHUNKS,)),
    ]
    vmem = pl.BlockSpec(memory_space=pltpu.VMEM)
    hbm = pl.BlockSpec(memory_space=pl.ANY)
    return pl.pallas_call(
        layer_kernel,
        out_shape=jax.ShapeDtypeStruct((rows, width), BF16),
        in_specs=[hbm] * 15,
        out_specs=vmem,
        scratch_shapes=scratch,
        compiler_params=pltpu.CompilerParams(
            collective_id=1, has_side_effects=True, vmem_limit_bytes=63 * 1024 * 1024
        ),
        cost_estimate=pl.CostEstimate(
            flops=20_000_000_000, bytes_accessed=20_000_000, transcendentals=9_000_000
        ),
        name="layer",
    )(
        queries,
        kv_latent,
        key_rope,
        w_key,
        w_value,
        w_out,
        residual,
        moe_gain,
        shared_gate.T,
        shared_up.T,
        shared_down,
        expert_gate_up,
        expert_down,
        expert_ids.T,
        gate_weights.T,
    )


def solution(mesh):
    in_specs = (
        P("ctx", "tp"),
        P(("ctx", "tp"), None),
        P(("ctx", "tp"), None),
        P(None, "tp"),
        P(None, "tp"),
        P("tp", None),
        P(("ctx", "tp"), None),
        P(),
        P(None, "tp"),
        P(None, "tp"),
        P("tp", None),
        P(("ctx", "tp"), None, None),
        P(("ctx", "tp"), None, None),
        P(("ctx", "tp"), None),
        P(("ctx", "tp"), None),
    )
    out_specs = P(("ctx", "tp"), None)
    return jax.shard_map(
        functools.partial(shards, mesh.shape["ctx"], mesh.shape["tp"]),
        mesh=mesh,
        in_specs=in_specs,
        out_specs=out_specs,
        check_vma=False,
    )
```

```python
import functools
import math

import jax
import jax.numpy as jnp
from jax import lax
from jax.experimental import pallas as pl
from jax.experimental.pallas import tpu as pltpu
from jax.sharding import PartitionSpec as P

NOPE = 128
ROPE = 64
VDIM = 128
TOPK = 6
CAP = 3
MESH = pl.DeviceIdType.MESH
F32 = jnp.float32
BF16 = jnp.bfloat16
LOW = -1e30
CHUNKS = 10
LEAD = 3
EARLY = 1


def loop(first, end, body):
    if isinstance(first, int) and isinstance(end, int):
        for i in range(first, end):
            body(i)
        return

    def step(i, carry):
        body(i)
        return carry

    lax.fori_loop(first, end, step, 0)


def dot(a, b):
    return jnp.dot(a, b, preferred_element_type=F32)


def dot_rows(a, b):
    return lax.dot_general(a, b, (((1,), (1,)), ((), ())), preferred_element_type=F32)


def layer_kernel(
    queries_hbm,
    kv_latent_hbm,
    key_rope_hbm,
    w_key_hbm,
    w_value_hbm,
    w_out_hbm,
    residual_hbm,
    gain_hbm,
    shared_gate_hbm,
    shared_up_hbm,
    shared_down_hbm,
    gate_up_hbm,
    down_hbm,
    ids_hbm,
    gates_hbm,
    out_ref,
    kv_latent,
    key_rope,
    ids_ref,
    gates_ref,
    queries,
    w_key,
    w_value,
    residual,
    gain,
    w_out,
    shared_gate,
    shared_up,
    shared_down,
    gate_up,
    down,
    load_sem,
    lat,
    q_s,
    k_s,
    v_s,
    top_s,
    acc_s,
    lat_ctx_send,
    lat_ctx_recv,
    lat_tp_send,
    lat_tp_recv,
    lat_sib_send,
    lat_sib_recv,
    part,
    sib_in,
    row_in,
    a_sib_send,
    a_sib_recv,
    a_row_send,
    a_row_recv,
    hidden,
    normed,
    n_send,
    n_recv,
    n_sib_send,
    n_sib_recv,
    pick,
    give,
    slots_out,
    slots_in,
    up_acc,
    x_send,
    x_recv,
    back_out,
    back_in,
    y_send,
    y_recv,
    shared_acc,
    part2,
    sib_in2,
    row_in2,
    b_sib_send,
    b_sib_recv,
    b_row_send,
    b_row_recv,
):
    c = lax.axis_index("ctx")
    t = lax.axis_index("tp")
    chip = t // 2
    core = t % 2
    other = 1 - core
    sibling = (c, chip * 2 + other)
    rows = residual.shape[0]
    width = residual.shape[1]
    heads = q_s.shape[0]
    latent = w_key.shape[0]
    n_ctx, _, n_chip = lat.shape[:3]
    half = n_chip * rows
    group = 2 * half
    span = width // CHUNKS
    slot_room = slots_out.shape[2]

    def cols(n):
        return pl.ds(n * span, span)

    def remote(src, dst, send, recv, device):
        return pltpu.make_async_remote_copy(
            src_ref=src,
            dst_ref=dst,
            send_sem=send,
            recv_sem=recv,
            device_id=device,
            device_id_type=MESH,
        )

    def chip_at(d):
        j = (chip + d) % n_chip
        return j, (c, j * 2 + core)

    def across(j):
        return ((j + c) % 2) * (n_chip // 2)

    def ctx_at(d):
        j = (c + d) % n_ctx
        return j, (j, ((chip + across(j)) % n_chip) * 2 + core)

    loads = []
    for i, (src, dst) in enumerate(
        (
            (kv_latent_hbm, kv_latent),
            (key_rope_hbm, key_rope),
            (ids_hbm, ids_ref),
            (gates_hbm, gates_ref),
            (queries_hbm, queries),
            (w_key_hbm, w_key),
            (w_value_hbm, w_value),
            (residual_hbm, residual),
            (gain_hbm, gain),
            (w_out_hbm, w_out),
            (shared_gate_hbm, shared_gate),
            (shared_up_hbm, shared_up),
            (shared_down_hbm, shared_down),
            (gate_up_hbm.at[0], gate_up),
            (down_hbm.at[0], down),
        )
    ):
        load = pltpu.make_async_copy(src, dst, load_sem.at[i])
        loads.append(load)
    for load in loads[:9]:
        load.start()
    loaded = set()

    def use(i):
        loaded.add(i)
        loads[i].wait()

    pending = []

    def finish():
        for i in range(len(loads)):
            if i not in loaded and (i < 9 or len(pending) > 1 or (pending and i < 10)):
                use(i)
        for wait in pending:
            wait()

    barrier = pltpu.get_barrier_semaphore()

    def greet(device):
        pl.semaphore_signal(barrier, inc=1, device_id=device, device_id_type=MESH)

    loop(1, n_chip, lambda d: greet(chip_at(d)[1]))
    loop(1, n_ctx, lambda d: greet(ctx_at(d)[1]))
    greet(sibling)
    pl.semaphore_wait(barrier, n_chip + n_ctx - 1)

    for i in range(4):
        use(i)
    lat[c, core, chip, :, :latent] = kv_latent[...]
    gates = gates_ref[...]
    gates_high = gates.astype(BF16).astype(F32)
    tail = jnp.concatenate(
        [
            jnp.zeros((ROPE, rows), F32),
            ids_ref[...].astype(F32),
            gates_high,
            gates - gates_high,
            jnp.zeros((ROPE - 3 * TOPK, rows), F32),
        ],
        axis=0,
    ).T
    lat[c, core, chip, :, latent:] = jnp.concatenate(
        [key_rope[...], tail[:, ROPE:].astype(BF16)], axis=1
    )

    def block_copy(s, d):
        held = (chip + across(s)) % n_chip
        return remote(
            lat.at[s, core, held],
            lat.at[s, core, held],
            lat_ctx_send.at[d],
            lat_ctx_recv.at[s],
            ctx_at(d)[1],
        )

    def half_copy(s, d):
        return remote(
            lat.at[s, core],
            lat.at[s, core],
            lat_ctx_send.at[d],
            lat_ctx_recv.at[s],
            ctx_at(d)[1],
        )

    odd = c % 2
    later = n_ctx - 1 - c
    earlier = c // 2
    passed = earlier + c // 4

    def each_later(whole, body):
        if whole:

            @pl.when(odd == 0)
            def _():
                body(1)

            for d in (6, 2):
                pl.when(later >= d)(functools.partial(body, d))
        else:
            loop(0, later // 2, lambda i: body(2 * (later // 2 - i) + 1 - 2 * odd))
            pl.when(later >= 4)(functools.partial(body, 4))

    def passed_back(i):
        return jnp.where(i <= earlier, 2 * i - 1 + 2 * odd, 4)

    def tp_copy(s, d):
        held = (chip + across(s)) % n_chip
        return remote(
            lat.at[s, core, held],
            lat.at[s, core, held],
            lat_tp_send.at[s],
            lat_tp_recv.at[s],
            chip_at(d)[1],
        )

    def tp_all(s):
        blocks = lat.at[s, core, pl.ds(0, n_chip - 1)]
        return remote(blocks, blocks, lat_tp_send.at[s], lat_tp_recv.at[s], sibling)

    loop(1, n_chip, lambda d: tp_copy(c, d).start())
    each_later(False, lambda d: block_copy(c, d).start())

    use(4)
    q_all = queries[...].reshape(n_chip, 2, rows, queries.shape[1])
    for k in range(2):
        q_half = q_all[:, k].reshape(half, queries.shape[1])
        for h in range(heads):
            piece = q_half[:, h * (NOPE + ROPE) : (h + 1) * (NOPE + ROPE)]
            q_s[h, k * half : (k + 1) * half, :] = jnp.concatenate(
                [piece, jnp.zeros((half, 2 * NOPE - NOPE - ROPE), BF16)], axis=1
            )
    top_s[...] = jnp.full(top_s.shape, LOW, F32)
    acc_s[...] = jnp.zeros(acc_s.shape, F32)

    def pass_on(i):
        s = c - passed_back(i)
        block_copy(s, 1).wait_recv()
        loop(1, n_chip, lambda d: tp_copy(s, d).start())

    loop(1, passed + 1, pass_on)

    def lat_sent():
        each_later(False, lambda d: block_copy(c, d).wait_send())
        each_later(True, lambda d: half_copy(c, d).wait_send())
        tp_all(c).wait_send()
        loop(1, passed + 1, lambda i: tp_all(c - passed_back(i)).wait_send())
        loop(0, c + 1, lambda i: sib_copy(c - i, core).wait_send())

    pending.append(lat_sent)

    scale = (1.0 / math.sqrt(NOPE + ROPE)) * math.log2(math.e)

    def place(index, axis_shape, axis):
        i = lax.broadcasted_iota(jnp.int32, axis_shape, axis) + index
        return ((i & (half - 1)) // rows) * (2 * rows) + (i // half) * rows + (i & (rows - 1))

    def attend(s, k=None):
        diagonal = k is not None
        block = lat[s, k] if diagonal else lat[s]
        block = block.reshape(-1, lat.shape[4])
        count = block.shape[0]
        k_s[:count] = dot(block[:, :latent], w_key[...]).astype(BF16)
        v_s[:count] = dot(block[:, :latent], w_value[...]).astype(BF16)
        rope = block[:, latent:]
        ones = jnp.ones((count, VDIM), BF16)
        if diagonal:
            query_at = place(0, (group, 128), 0)
            query_at = jnp.concatenate([query_at] * (count // 128), axis=1)
            key_at = place(k * half, (8, count), 1)[:1]
        for h in range(heads):
            keys = jnp.concatenate([k_s[:count, h * NOPE : (h + 1) * NOPE], rope], axis=1)
            values = jnp.concatenate([v_s[:count, h * VDIM : (h + 1) * VDIM], ones], axis=1)
            scores = dot_rows(q_s[h], keys)
            if diagonal:
                scores = jnp.where(key_at <= query_at, scores, LOW)
            top_old = top_s[h]
            top_new = jnp.maximum(top_old, jnp.max(scores, axis=1, keepdims=True))
            top_s[h] = top_new
            weights = jnp.concatenate(
                [
                    jnp.exp2((scores[:, j * 128 : (j + 1) * 128] - top_new) * scale).astype(BF16)
                    for j in range(count // 128)
                ],
                axis=1,
            )
            factor = jnp.exp2((top_old - top_new) * scale)
            factor = jnp.concatenate([factor, factor], axis=1)
            acc_s[h] = acc_s[h] * factor + dot(weights, values)

    def sib_copy(s, k):
        return remote(lat.at[s, k], lat.at[s, k], lat_sib_send.at[s], lat_sib_recv.at[s], sibling)

    ahead = jnp.minimum(passed, EARLY)
    halves = c - passed

    def block_at(q):
        whole = jnp.where(q <= ahead, 0, jnp.where(q <= ahead + halves, 1, 0))
        r = q - ahead
        half_back = jnp.where(r <= odd, 1, 4 * (r - odd) - 2)
        i = jnp.where(q <= ahead, q, q - halves)
        return c - jnp.where(whole == 1, half_back, passed_back(i)), whole

    tp_all(c).wait_recv()
    each_later(True, lambda d: half_copy(c, d).start())
    sib_copy(c, core).start()
    use(5)
    use(6)

    def own_step(j):
        @pl.when(j == 1)
        def _():
            sib_copy(c, other).wait_recv()

        attend(c, (core + j) % 2)

    loop(0, jnp.minimum(2, c + 2), own_step)
    loads[9].start()

    def key_step(q):
        s, whole = block_at(q)

        @pl.when((q <= c) & (whole == 0))
        def _():
            tp_all(s).wait_recv()

        @pl.when((q <= c) & (whole == 1))
        def _():
            half_copy(s, 2).wait_recv()

        @pl.when(q <= c)
        def _():
            sib_copy(s, core).start()

        @pl.when(q > 1)
        def _():
            attend(block_at(q - 1)[0])

        @pl.when(q <= c)
        def _():
            sib_copy(s, other).wait_recv()

    loop(1, c + 2, key_step)

    def sib_part(n, buffer, landing, send, recv):
        return remote(
            buffer.at[n, other],
            landing.at[n],
            send.at[0],
            recv.at[n],
            sibling,
        )

    def row_part(n, d, buffer, landing, send, recv):
        j, device = chip_at(d)
        return remote(
            buffer.at[n, core, j],
            landing.at[n, chip],
            send.at[0],
            recv.at[n],
            device,
        )

    def pass_rows(n, buffer, from_sibling, landing, sib_send, sib_recv, send, recv):
        sib_part(n, buffer, from_sibling, sib_send, sib_recv).wait_recv()
        summed = (
            buffer[n, core].astype(F32) + from_sibling[n].astype(F32)
        ).astype(BF16)
        buffer[n, core] = summed
        landing[n, chip] = buffer[n, core, chip]
        loop(1, n_chip, lambda d: row_part(n, d, buffer, landing, send, recv).start())

    def rows_sent(buffer, from_sibling, landing, sib_send, sib_recv, send, recv):
        remote(
            buffer.at[:, other], from_sibling, sib_send.at[0], sib_recv.at[0], sibling
        ).wait_send()
        others = pl.ds(0, n_chip - 1)
        remote(
            buffer.at[:, core, others], landing.at[:, others], send.at[0], recv.at[0], sibling
        ).wait_send()

    def sum_rows(n, landing, send, recv):
        blocks = landing.at[n, pl.ds(0, n_chip - 1)]
        remote(blocks, blocks, send.at[0], recv.at[n], sibling).wait_recv()
        return jnp.sum(landing[n].astype(F32), axis=0)

    attention = jnp.concatenate(
        [(acc_s[h, :, :VDIM] / acc_s[h, :, VDIM:]).astype(BF16) for h in range(heads)], axis=1
    )
    use(9)
    first = (part, sib_in, row_in, a_sib_send, a_sib_recv, a_row_send, a_row_recv)
    for n in range(CHUNKS):
        part[n] = (
            dot(attention, w_out[:, cols(n)]).astype(BF16).reshape(2, n_chip, rows, span)
        )
        sib_part(n, part, sib_in, a_sib_send, a_sib_recv).start()
        if n > 0:
            pass_rows(n - 1, *first)
    pass_rows(CHUNKS - 1, *first)
    pending.append(functools.partial(rows_sent, *first))

    for load in loads[10:]:
        load.start()

    meta = lat[c, :, :, :, latent:].reshape(group, lat.shape[4] - latent).astype(F32).T
    ids = meta[ROPE : ROPE + TOPK]
    gates_all = meta[ROPE + TOPK : ROPE + 2 * TOPK] + meta[ROPE + 2 * TOPK : ROPE + 3 * TOPK]
    expert_row = lax.broadcasted_iota(jnp.int32, (16, group), 0)
    owner = expert_row * (2 * n_chip) + ((chip + across(expert_row)) % n_chip) * 2 + core
    expert = jnp.where(expert_row < n_ctx, owner, -1).astype(F32)
    member = jnp.zeros((16, group), F32)
    gate = jnp.zeros((16, group), F32)
    for k in range(TOPK):
        same = ids[k : k + 1] == expert
        member = member + jnp.where(same, 1.0, 0.0)
        gate = gate + jnp.where(same, gates_all[k : k + 1], 0.0)
    before = lax.broadcasted_iota(jnp.int32, (group, group), 0) < lax.broadcasted_iota(
        jnp.int32, (group, group), 1
    )
    rank = dot(member.astype(BF16), jnp.where(before, 1.0, 0.0).astype(BF16))
    slot = lax.broadcasted_iota(jnp.int32, (slot_room, group), 0).astype(F32)
    for e in range(n_ctx):
        chosen = jnp.where(member[e : e + 1] > 0.5, rank[e : e + 1], -1.0) == slot
        pick[e] = jnp.where(chosen, 1.0, 0.0).astype(BF16)
        give[e] = jnp.where(chosen, gate[e : e + 1], 0.0).astype(BF16)

    def normed_copy(n, d):
        block = normed.at[n, core, chip]
        return remote(block, block, n_send.at[0], n_recv.at[n], chip_at(d)[1])

    def normed_all(n):
        blocks = normed.at[n, core, pl.ds(0, n_chip - 1)]
        return remote(blocks, blocks, n_send.at[0], n_recv.at[n], sibling)

    def normed_sib(n):
        half_rows = normed.at[n, core]
        return remote(half_rows, half_rows, n_sib_send.at[0], n_sib_recv.at[n], sibling)

    def normed_sent():
        blocks = normed.at[:, core, pl.ds(0, n_chip - 1)]
        remote(blocks, blocks, n_send.at[0], n_recv.at[0], sibling).wait_send()
        half_rows = normed.at[:, core]
        remote(half_rows, half_rows, n_sib_send.at[0], n_sib_recv.at[0], sibling).wait_send()

    def send_rows(n):
        state = residual[:, cols(n)].astype(F32) + sum_rows(n, row_in, a_row_send, a_row_recv)
        hidden[:, cols(n)] = state
        normed[n, core, chip] = (state * gain[cols(n)].reshape(1, span)).astype(BF16)
        loop(1, n_chip, lambda d: normed_copy(n, d).start())

    def square_sum(block, n):
        plain = block.astype(F32) * (1.0 / gain[cols(n)].reshape(1, span))
        return jnp.sum(plain * plain, axis=1, keepdims=True)

    def norm_factor(total):
        return lax.rsqrt(total * (1.0 / width) + 1e-06)

    use(7)
    use(8)
    for n in range(LEAD):
        send_rows(n)
    pending.append(normed_sent)

    def slot_copy(n, d, source, landing, send, recv):
        j, device = ctx_at(d)
        return remote(
            source.at[n, j], landing.at[n, c], send.at[0], recv.at[n], device
        )

    def slot_wait(n, source, landing, send, recv):
        blocks = landing.at[n, pl.ds(0, n_ctx - 1)]
        remote(blocks, blocks, send.at[0], recv.at[n], sibling).wait_recv()

    def slots_sent(source, landing, send, recv):
        blocks = source.at[:, pl.ds(0, n_ctx - 1)]
        remote(blocks, blocks, send.at[0], recv.at[0], sibling).wait_send()

    there = (slots_out, slots_in, x_send, x_recv)
    back = (back_out, back_in, y_send, y_recv)
    def dispatch(n):
        normed_sib(n).wait_recv()
        block = normed[n].reshape(group, span)
        picked = dot(pick[...].reshape(n_ctx * slot_room, group), block).astype(BF16)
        slots_out[n] = picked.reshape(n_ctx, slot_room, span)
        loop(1, n_ctx, lambda d: slot_copy(n, d, *there).start())
        slots_in[n, c] = slots_out[n, c]

    for n in range(CHUNKS):
        if n + LEAD < CHUNKS:
            send_rows(n + LEAD)
        normed_all(n).wait_recv()
        normed_sib(n).start()
        if n > 0:
            dispatch(n - 1)
    dispatch(CHUNKS - 1)
    pending.append(functools.partial(slots_sent, *there))

    use(10)
    use(11)
    group_squares = 0.0
    gate_sum = 0.0
    up_sum = 0.0
    for n in range(CHUNKS):
        block = normed[n].reshape(group, span)
        group_squares = group_squares + square_sum(block, n)
        gate_sum = gate_sum + dot_rows(block, shared_gate[:, cols(n)])
        up_sum = up_sum + dot_rows(block, shared_up[:, cols(n)])
    factor = norm_factor(group_squares)
    gate_part = gate_sum * factor
    up_part = up_sum * factor
    shared_hidden = (gate_part / (1.0 + jnp.exp(-gate_part)) * up_part).astype(BF16)
    use(12)
    for n in range(CHUNKS):
        shared_acc[:, cols(n)] = dot(shared_hidden, shared_down[:, cols(n)])

    use(13)
    use(14)
    slot_squares = 0.0
    for n in range(CHUNKS):
        slot_wait(n, *there)
        items = slots_in[n].reshape(n_ctx * slot_room, span)
        product = dot(items, gate_up[cols(n), :])
        slot_squares = slot_squares + square_sum(items, n)
        if n == 0:
            up_acc[...] = product
        else:
            up_acc[...] = up_acc[...] + product
    inner = down.shape[0]
    factor = norm_factor(slot_squares)
    gate_part = up_acc[:, :inner] * factor
    up_part = up_acc[:, inner:] * factor
    expert_hidden = (gate_part / (1.0 + jnp.exp(-gate_part)) * up_part).astype(BF16)
    for n in range(CHUNKS):
        result = dot(expert_hidden, down[:, cols(n)]).astype(BF16)
        back_out[n] = result.reshape(n_ctx, slot_room, span)
        loop(1, n_ctx, lambda d: slot_copy(n, d, *back).start())
        back_in[n, c] = back_out[n, c]
    pending.append(functools.partial(slots_sent, *back))

    give_rows = give[...].reshape(n_ctx * slot_room, group).astype(F32).T.astype(BF16)
    second = (part2, sib_in2, row_in2, b_sib_send, b_sib_recv, b_row_send, b_row_recv)
    for n in range(CHUNKS):
        slot_wait(n, *back)
        returned = back_in[n].reshape(n_ctx * slot_room, span)
        both = shared_acc[:, cols(n)] + dot(give_rows, returned)
        part2[n] = both.astype(BF16).reshape(2, n_chip, rows, span)
        sib_part(n, part2, sib_in2, b_sib_send, b_sib_recv).start()
        if n > 0:
            pass_rows(n - 1, *second)
    pass_rows(CHUNKS - 1, *second)
    pending.append(functools.partial(rows_sent, *second))
    for n in range(CHUNKS):
        out_ref[:, cols(n)] = (
            hidden[:, cols(n)] + sum_rows(n, row_in2, b_row_send, b_row_recv)
        )

    finish()


def shards(
    n_ctx,
    n_tp,
    queries,
    kv_latent,
    key_rope,
    w_key,
    w_value,
    w_out,
    residual,
    moe_gain,
    shared_gate,
    shared_up,
    shared_down,
    expert_gate_up,
    expert_down,
    expert_ids,
    gate_weights,
):
    rows, width = residual.shape
    n_chip = n_tp // 2
    heads = w_key.shape[1] // NOPE
    group = rows * n_tp
    latent = kv_latent.shape[1]
    slot_room = CAP * n_tp
    dma = pltpu.SemaphoreType.DMA
    scratch = [
        pltpu.VMEM(kv_latent.shape, BF16),
        pltpu.VMEM(key_rope.shape, BF16),
        pltpu.VMEM(expert_ids.shape[::-1], jnp.int32),
        pltpu.VMEM(gate_weights.shape[::-1], F32),
        pltpu.VMEM(queries.shape, BF16),
        pltpu.VMEM(w_key.shape, BF16),
        pltpu.VMEM(w_value.shape, BF16),
        pltpu.VMEM(residual.shape, BF16),
        pltpu.VMEM(moe_gain.shape, F32),
        pltpu.VMEM(w_out.shape, BF16),
        pltpu.VMEM(shared_gate.shape[::-1], BF16),
        pltpu.VMEM(shared_up.shape[::-1], BF16),
        pltpu.VMEM(shared_down.shape, BF16),
        pltpu.VMEM(expert_gate_up.shape[1:], BF16),
        pltpu.VMEM(expert_down.shape[1:], BF16),
        dma((15,)),
        pltpu.VMEM((n_ctx, 2, n_chip, rows, latent + 128), BF16),
        pltpu.VMEM((heads, group, 2 * NOPE), BF16),
        pltpu.VMEM((group, heads * NOPE), BF16),
        pltpu.VMEM((group, heads * VDIM), BF16),
        pltpu.VMEM((heads, group, 128), F32),
        pltpu.VMEM((heads, group, 2 * VDIM), F32),
        dma((n_ctx,)),
        dma((n_ctx,)),
        dma((n_ctx,)),
        dma((n_ctx,)),
        dma((n_ctx,)),
        dma((n_ctx,)),
        pltpu.VMEM((CHUNKS, 2, n_chip, rows, width // CHUNKS), BF16),
        pltpu.VMEM((CHUNKS, n_chip, rows, width // CHUNKS), BF16),
        pltpu.VMEM((CHUNKS, n_chip, rows, width // CHUNKS), BF16),
        dma((1,)),
        dma((CHUNKS,)),
        dma((1,)),
        dma((CHUNKS,)),
        pltpu.VMEM((rows, width), F32),
        pltpu.VMEM((CHUNKS, 2, n_chip, rows, width // CHUNKS), BF16),
        dma((1,)),
        dma((CHUNKS,)),
        dma((1,)),
        dma((CHUNKS,)),
        pltpu.VMEM((n_ctx, slot_room, group), BF16),
        pltpu.VMEM((n_ctx, slot_room, group), BF16),
        pltpu.VMEM((CHUNKS, n_ctx, slot_room, width // CHUNKS), BF16),
        pltpu.VMEM((CHUNKS, n_ctx, slot_room, width // CHUNKS), BF16),
        pltpu.VMEM((n_ctx * slot_room, expert_gate_up.shape[2]), F32),
        dma((1,)),
        dma((CHUNKS,)),
        pltpu.VMEM((CHUNKS, n_ctx, slot_room, width // CHUNKS), BF16),
        pltpu.VMEM((CHUNKS, n_ctx, slot_room, width // CHUNKS), BF16),
        dma((1,)),
        dma((CHUNKS,)),
        pltpu.VMEM((group, width), F32),
        pltpu.VMEM((CHUNKS, 2, n_chip, rows, width // CHUNKS), BF16),
        pltpu.VMEM((CHUNKS, n_chip, rows, width // CHUNKS), BF16),
        pltpu.VMEM((CHUNKS, n_chip, rows, width // CHUNKS), BF16),
        dma((1,)),
        dma((CHUNKS,)),
        dma((1,)),
        dma((CHUNKS,)),
    ]
    vmem = pl.BlockSpec(memory_space=pltpu.VMEM)
    hbm = pl.BlockSpec(memory_space=pl.ANY)
    return pl.pallas_call(
        layer_kernel,
        out_shape=jax.ShapeDtypeStruct((rows, width), F32),
        in_specs=[hbm] * 15,
        out_specs=vmem,
        scratch_shapes=scratch,
        compiler_params=pltpu.CompilerParams(
            collective_id=1, has_side_effects=True, vmem_limit_bytes=63 * 1024 * 1024
        ),
        cost_estimate=pl.CostEstimate(
            flops=20_000_000_000, bytes_accessed=20_000_000, transcendentals=9_000_000
        ),
        name="layer",
    )(
        queries,
        kv_latent,
        key_rope,
        w_key,
        w_value,
        w_out,
        residual,
        moe_gain,
        shared_gate.T,
        shared_up.T,
        shared_down,
        expert_gate_up,
        expert_down,
        expert_ids.T,
        gate_weights.T,
    ).astype(BF16)


def solution(mesh):
    in_specs = (
        P("ctx", "tp"),
        P(("ctx", "tp"), None),
        P(("ctx", "tp"), None),
        P(None, "tp"),
        P(None, "tp"),
        P("tp", None),
        P(("ctx", "tp"), None),
        P(),
        P(None, "tp"),
        P(None, "tp"),
        P("tp", None),
        P(("ctx", "tp"), None, None),
        P(("ctx", "tp"), None, None),
        P(("ctx", "tp"), None),
        P(("ctx", "tp"), None),
    )
    out_specs = P(("ctx", "tp"), None)
    return jax.shard_map(
        functools.partial(shards, mesh.shape["ctx"], mesh.shape["tp"]),
        mesh=mesh,
        in_specs=in_specs,
        out_specs=out_specs,
        check_vma=False,
    )
```

```python
import functools
import math

import jax
import jax.numpy as jnp
from jax import lax
from jax.experimental import pallas as pl
from jax.experimental.pallas import tpu as pltpu
from jax.sharding import PartitionSpec as P

NOPE = 128
ROPE = 64
VDIM = 128
TOPK = 6
CAP = 3
MESH = pl.DeviceIdType.MESH
F32 = jnp.float32
BF16 = jnp.bfloat16
LOW = -1e30
CHUNKS = 10
LEAD = 3
EARLY = 1


def loop(first, end, body):
    if isinstance(first, int) and isinstance(end, int):
        for i in range(first, end):
            body(i)
        return

    def step(i, carry):
        body(i)
        return carry

    lax.fori_loop(first, end, step, 0)


def dot(a, b):
    return jnp.dot(a, b, preferred_element_type=F32)


def dot_rows(a, b):
    return lax.dot_general(a, b, (((1,), (1,)), ((), ())), preferred_element_type=F32)


def layer_kernel(
    queries_hbm,
    kv_latent_hbm,
    key_rope_hbm,
    w_key_hbm,
    w_value_hbm,
    w_out_hbm,
    residual_hbm,
    gain_hbm,
    shared_gate_hbm,
    shared_up_hbm,
    shared_down_hbm,
    gate_up_hbm,
    down_hbm,
    ids_hbm,
    gates_hbm,
    out_ref,
    kv_latent,
    key_rope,
    ids_ref,
    gates_ref,
    queries,
    w_key,
    w_value,
    residual,
    gain,
    w_out,
    shared_gate,
    shared_up,
    shared_down,
    gate_up,
    down,
    load_sem,
    lat,
    q_s,
    k_s,
    v_s,
    top_s,
    acc_s,
    lat_ctx_send,
    lat_ctx_recv,
    lat_tp_send,
    lat_tp_recv,
    lat_sib_send,
    lat_sib_recv,
    part,
    sib_in,
    row_in,
    a_sib_send,
    a_sib_recv,
    a_row_send,
    a_row_recv,
    hidden,
    normed,
    n_send,
    n_recv,
    n_sib_send,
    n_sib_recv,
    pick,
    give,
    slots_out,
    slots_in,
    up_acc,
    x_send,
    x_recv,
    back_out,
    back_in,
    y_send,
    y_recv,
    part2,
    sib_in2,
    row_in2,
    b_sib_send,
    b_sib_recv,
    b_row_send,
    b_row_recv,
):
    c = lax.axis_index("ctx")
    t = lax.axis_index("tp")
    chip = t // 2
    core = t % 2
    other = 1 - core
    sibling = (c, chip * 2 + other)
    rows = residual.shape[0]
    width = residual.shape[1]
    heads = q_s.shape[0]
    latent = w_key.shape[0]
    n_ctx, _, n_chip = lat.shape[:3]
    half = n_chip * rows
    group = 2 * half
    span = width // CHUNKS
    slot_room = slots_out.shape[2]

    def cols(n):
        return pl.ds(n * span, span)

    def remote(src, dst, send, recv, device):
        return pltpu.make_async_remote_copy(
            src_ref=src,
            dst_ref=dst,
            send_sem=send,
            recv_sem=recv,
            device_id=device,
            device_id_type=MESH,
        )

    def chip_at(d):
        j = (chip + d) % n_chip
        return j, (c, j * 2 + core)

    def across(j):
        return ((j + c) % 2) * (n_chip // 2)

    def ctx_at(d):
        j = (c + d) % n_ctx
        return j, (j, ((chip + across(j)) % n_chip) * 2 + core)

    loads = []
    for i, (src, dst) in enumerate(
        (
            (kv_latent_hbm, kv_latent),
            (key_rope_hbm, key_rope),
            (ids_hbm, ids_ref),
            (gates_hbm, gates_ref),
            (queries_hbm, queries),
            (w_key_hbm, w_key),
            (w_value_hbm, w_value),
            (residual_hbm, residual),
            (gain_hbm, gain),
            (w_out_hbm, w_out),
            (shared_gate_hbm, shared_gate),
            (shared_up_hbm, shared_up),
            (shared_down_hbm, shared_down),
            (gate_up_hbm.at[0], gate_up),
            (down_hbm.at[0], down),
        )
    ):
        load = pltpu.make_async_copy(src, dst, load_sem.at[i])
        loads.append(load)
    for load in loads[:9]:
        load.start()
    loaded = set()

    def use(i):
        loaded.add(i)
        loads[i].wait()

    pending = []

    def finish():
        for i in range(len(loads)):
            if i not in loaded and (i < 9 or len(pending) > 1 or (pending and i < 10)):
                use(i)
        for wait in pending:
            wait()

    barrier = pltpu.get_barrier_semaphore()

    def greet(device):
        pl.semaphore_signal(barrier, inc=1, device_id=device, device_id_type=MESH)

    loop(1, n_chip, lambda d: greet(chip_at(d)[1]))
    loop(1, n_ctx, lambda d: greet(ctx_at(d)[1]))
    greet(sibling)
    pl.semaphore_wait(barrier, n_chip + n_ctx - 1)

    for i in range(4):
        use(i)
    lat[c, core, chip, :, :latent] = kv_latent[...]
    gates = gates_ref[...]
    gates_high = gates.astype(BF16).astype(F32)
    tail = jnp.concatenate(
        [
            jnp.zeros((ROPE, rows), F32),
            ids_ref[...].astype(F32),
            gates_high,
            gates - gates_high,
            jnp.zeros((ROPE - 3 * TOPK, rows), F32),
        ],
        axis=0,
    ).T
    lat[c, core, chip, :, latent:] = jnp.concatenate(
        [key_rope[...], tail[:, ROPE:].astype(BF16)], axis=1
    )

    def block_copy(s, d):
        held = (chip + across(s)) % n_chip
        return remote(
            lat.at[s, core, held],
            lat.at[s, core, held],
            lat_ctx_send.at[d],
            lat_ctx_recv.at[s],
            ctx_at(d)[1],
        )

    def half_copy(s, d):
        return remote(
            lat.at[s, core],
            lat.at[s, core],
            lat_ctx_send.at[d],
            lat_ctx_recv.at[s],
            ctx_at(d)[1],
        )

    odd = c % 2
    later = n_ctx - 1 - c
    earlier = c // 2
    passed = earlier + c // 4

    def each_later(whole, body):
        if whole:

            @pl.when(odd == 0)
            def _():
                body(1)

            for d in (6, 2):
                pl.when(later >= d)(functools.partial(body, d))
        else:
            loop(0, later // 2, lambda i: body(2 * (later // 2 - i) + 1 - 2 * odd))
            pl.when(later >= 4)(functools.partial(body, 4))

    def passed_back(i):
        return jnp.where(i <= earlier, 2 * i - 1 + 2 * odd, 4)

    def tp_copy(s, d):
        held = (chip + across(s)) % n_chip
        return remote(
            lat.at[s, core, held],
            lat.at[s, core, held],
            lat_tp_send.at[s],
            lat_tp_recv.at[s],
            chip_at(d)[1],
        )

    def tp_all(s):
        blocks = lat.at[s, core, pl.ds(0, n_chip - 1)]
        return remote(blocks, blocks, lat_tp_send.at[s], lat_tp_recv.at[s], sibling)

    loop(1, n_chip, lambda d: tp_copy(c, d).start())
    each_later(False, lambda d: block_copy(c, d).start())

    use(4)
    q_all = queries[...].reshape(n_chip, 2, rows, queries.shape[1])
    for k in range(2):
        q_half = q_all[:, k].reshape(half, queries.shape[1])
        for h in range(heads):
            piece = q_half[:, h * (NOPE + ROPE) : (h + 1) * (NOPE + ROPE)]
            q_s[h, k * half : (k + 1) * half, :] = jnp.concatenate(
                [piece, jnp.zeros((half, 2 * NOPE - NOPE - ROPE), BF16)], axis=1
            )
    top_s[...] = jnp.full(top_s.shape, LOW, F32)
    acc_s[...] = jnp.zeros(acc_s.shape, F32)

    def pass_on(i):
        s = c - passed_back(i)
        block_copy(s, 1).wait_recv()
        loop(1, n_chip, lambda d: tp_copy(s, d).start())

    loop(1, passed + 1, pass_on)

    def lat_sent():
        each_later(False, lambda d: block_copy(c, d).wait_send())
        each_later(True, lambda d: half_copy(c, d).wait_send())
        tp_all(c).wait_send()
        loop(1, passed + 1, lambda i: tp_all(c - passed_back(i)).wait_send())
        loop(0, c + 1, lambda i: sib_copy(c - i, core).wait_send())

    pending.append(lat_sent)

    scale = (1.0 / math.sqrt(NOPE + ROPE)) * math.log2(math.e)

    def place(index, axis_shape, axis):
        i = lax.broadcasted_iota(jnp.int32, axis_shape, axis) + index
        return ((i & (half - 1)) // rows) * (2 * rows) + (i // half) * rows + (i & (rows - 1))

    def attend(s, k=None):
        diagonal = k is not None
        block = lat[s, k] if diagonal else lat[s]
        block = block.reshape(-1, lat.shape[4])
        count = block.shape[0]
        k_s[:count] = dot(block[:, :latent], w_key[...]).astype(BF16)
        v_s[:count] = dot(block[:, :latent], w_value[...]).astype(BF16)
        rope = block[:, latent:]
        ones = jnp.ones((count, VDIM), BF16)
        if diagonal:
            query_at = place(0, (group, 128), 0)
            query_at = jnp.concatenate([query_at] * (count // 128), axis=1)
            key_at = place(k * half, (8, count), 1)[:1]
        for h in range(heads):
            keys = jnp.concatenate([k_s[:count, h * NOPE : (h + 1) * NOPE], rope], axis=1)
            values = jnp.concatenate([v_s[:count, h * VDIM : (h + 1) * VDIM], ones], axis=1)
            scores = dot_rows(q_s[h], keys)
            if diagonal:
                scores = jnp.where(key_at <= query_at, scores, LOW)
            top_old = top_s[h]
            top_new = jnp.maximum(top_old, jnp.max(scores, axis=1, keepdims=True))
            top_s[h] = top_new
            weights = jnp.concatenate(
                [
                    jnp.exp2((scores[:, j * 128 : (j + 1) * 128] - top_new) * scale).astype(BF16)
                    for j in range(count // 128)
                ],
                axis=1,
            )
            factor = jnp.exp2((top_old - top_new) * scale)
            factor = jnp.concatenate([factor, factor], axis=1)
            acc_s[h] = acc_s[h] * factor + dot(weights, values)

    def sib_copy(s, k):
        return remote(lat.at[s, k], lat.at[s, k], lat_sib_send.at[s], lat_sib_recv.at[s], sibling)

    ahead = jnp.minimum(passed, EARLY)
    halves = c - passed

    def block_at(q):
        whole = jnp.where(q <= ahead, 0, jnp.where(q <= ahead + halves, 1, 0))
        r = q - ahead
        half_back = jnp.where(r <= odd, 1, 4 * (r - odd) - 2)
        i = jnp.where(q <= ahead, q, q - halves)
        return c - jnp.where(whole == 1, half_back, passed_back(i)), whole

    tp_all(c).wait_recv()
    each_later(True, lambda d: half_copy(c, d).start())
    sib_copy(c, core).start()
    use(5)
    use(6)

    def own_step(j):
        @pl.when(j == 1)
        def _():
            sib_copy(c, other).wait_recv()

        attend(c, (core + j) % 2)

    loop(0, jnp.minimum(2, c + 2), own_step)
    loads[9].start()

    def key_step(q):
        s, whole = block_at(q)

        @pl.when((q <= c) & (whole == 0))
        def _():
            tp_all(s).wait_recv()

        @pl.when((q <= c) & (whole == 1))
        def _():
            half_copy(s, 2).wait_recv()

        @pl.when(q <= c)
        def _():
            sib_copy(s, core).start()

        @pl.when(q > 1)
        def _():
            attend(block_at(q - 1)[0])

        @pl.when(q <= c)
        def _():
            sib_copy(s, other).wait_recv()

    loop(1, c + 2, key_step)

    def sib_part(n, buffer, landing, send, recv):
        return remote(
            buffer.at[n, other],
            landing.at[n],
            send.at[0],
            recv.at[n],
            sibling,
        )

    def row_part(n, d, buffer, landing, send, recv):
        j, device = chip_at(d)
        return remote(
            buffer.at[n, core, j],
            landing.at[n, chip],
            send.at[0],
            recv.at[n],
            device,
        )

    def pass_rows(n, buffer, from_sibling, landing, sib_send, sib_recv, send, recv):
        sib_part(n, buffer, from_sibling, sib_send, sib_recv).wait_recv()
        summed = (
            buffer[n, core].astype(F32) + from_sibling[n].astype(F32)
        ).astype(BF16)
        buffer[n, core] = summed
        landing[n, chip] = buffer[n, core, chip]
        loop(1, n_chip, lambda d: row_part(n, d, buffer, landing, send, recv).start())

    def rows_sent(buffer, from_sibling, landing, sib_send, sib_recv, send, recv):
        remote(
            buffer.at[:, other], from_sibling, sib_send.at[0], sib_recv.at[0], sibling
        ).wait_send()
        others = pl.ds(0, n_chip - 1)
        remote(
            buffer.at[:, core, others], landing.at[:, others], send.at[0], recv.at[0], sibling
        ).wait_send()

    def sum_rows(n, landing, send, recv):
        blocks = landing.at[n, pl.ds(0, n_chip - 1)]
        remote(blocks, blocks, send.at[0], recv.at[n], sibling).wait_recv()
        return jnp.sum(landing[n].astype(F32), axis=0)

    attention = jnp.concatenate(
        [(acc_s[h, :, :VDIM] / acc_s[h, :, VDIM:]).astype(BF16) for h in range(heads)], axis=1
    )
    use(9)
    first = (part, sib_in, row_in, a_sib_send, a_sib_recv, a_row_send, a_row_recv)
    for n in range(CHUNKS):
        part[n] = (
            dot(attention, w_out[:, cols(n)]).astype(BF16).reshape(2, n_chip, rows, span)
        )
        sib_part(n, part, sib_in, a_sib_send, a_sib_recv).start()
        if n > 0:
            pass_rows(n - 1, *first)
    pass_rows(CHUNKS - 1, *first)
    pending.append(functools.partial(rows_sent, *first))

    for load in loads[10:]:
        load.start()

    meta = lat[c, :, :, :, latent:].reshape(group, lat.shape[4] - latent).astype(F32).T
    ids = meta[ROPE : ROPE + TOPK]
    gates_all = meta[ROPE + TOPK : ROPE + 2 * TOPK] + meta[ROPE + 2 * TOPK : ROPE + 3 * TOPK]
    expert_row = lax.broadcasted_iota(jnp.int32, (16, group), 0)
    owner = expert_row * (2 * n_chip) + ((chip + across(expert_row)) % n_chip) * 2 + core
    expert = jnp.where(expert_row < n_ctx, owner, -1).astype(F32)
    member = jnp.zeros((16, group), F32)
    gate = jnp.zeros((16, group), F32)
    for k in range(TOPK):
        same = ids[k : k + 1] == expert
        member = member + jnp.where(same, 1.0, 0.0)
        gate = gate + jnp.where(same, gates_all[k : k + 1], 0.0)
    before = lax.broadcasted_iota(jnp.int32, (group, group), 0) < lax.broadcasted_iota(
        jnp.int32, (group, group), 1
    )
    rank = dot(member.astype(BF16), jnp.where(before, 1.0, 0.0).astype(BF16))
    slot = lax.broadcasted_iota(jnp.int32, (slot_room, group), 0).astype(F32)
    for e in range(n_ctx):
        chosen = jnp.where(member[e : e + 1] > 0.5, rank[e : e + 1], -1.0) == slot
        pick[e] = jnp.where(chosen, 1.0, 0.0).astype(BF16)
        give[e] = jnp.where(chosen, gate[e : e + 1], 0.0).astype(BF16)

    def normed_copy(n, d):
        block = normed.at[n, core, chip]
        return remote(block, block, n_send.at[0], n_recv.at[n], chip_at(d)[1])

    def normed_all(n):
        blocks = normed.at[n, core, pl.ds(0, n_chip - 1)]
        return remote(blocks, blocks, n_send.at[0], n_recv.at[n], sibling)

    def normed_sib(n):
        half_rows = normed.at[n, core]
        return remote(half_rows, half_rows, n_sib_send.at[0], n_sib_recv.at[n], sibling)

    def normed_sent():
        blocks = normed.at[:, core, pl.ds(0, n_chip - 1)]
        remote(blocks, blocks, n_send.at[0], n_recv.at[0], sibling).wait_send()
        half_rows = normed.at[:, core]
        remote(half_rows, half_rows, n_sib_send.at[0], n_sib_recv.at[0], sibling).wait_send()

    def send_rows(n):
        state = residual[:, cols(n)].astype(F32) + sum_rows(n, row_in, a_row_send, a_row_recv)
        hidden[:, cols(n)] = state
        normed[n, core, chip] = (state * gain[cols(n)].reshape(1, span)).astype(BF16)
        loop(1, n_chip, lambda d: normed_copy(n, d).start())

    def square_sum(block, n):
        plain = block.astype(F32) * (1.0 / gain[cols(n)].reshape(1, span))
        return jnp.sum(plain * plain, axis=1, keepdims=True)

    def norm_factor(total):
        return lax.rsqrt(total * (1.0 / width) + 1e-06)

    use(7)
    use(8)
    for n in range(LEAD):
        send_rows(n)
    pending.append(normed_sent)

    def slot_copy(n, d, source, landing, send, recv):
        j, device = ctx_at(d)
        return remote(
            source.at[n, j], landing.at[n, c], send.at[0], recv.at[n], device
        )

    def slot_wait(n, source, landing, send, recv):
        blocks = landing.at[n, pl.ds(0, n_ctx - 1)]
        remote(blocks, blocks, send.at[0], recv.at[n], sibling).wait_recv()

    def slots_sent(source, landing, send, recv):
        blocks = source.at[:, pl.ds(0, n_ctx - 1)]
        remote(blocks, blocks, send.at[0], recv.at[0], sibling).wait_send()

    there = (slots_out, slots_in, x_send, x_recv)
    back = (back_out, back_in, y_send, y_recv)
    def dispatch(n):
        normed_sib(n).wait_recv()
        block = normed[n].reshape(group, span)
        picked = dot(pick[...].reshape(n_ctx * slot_room, group), block).astype(BF16)
        slots_out[n] = picked.reshape(n_ctx, slot_room, span)
        loop(1, n_ctx, lambda d: slot_copy(n, d, *there).start())
        slots_in[n, c] = slots_out[n, c]

    for n in range(CHUNKS):
        if n + LEAD < CHUNKS:
            send_rows(n + LEAD)
        normed_all(n).wait_recv()
        normed_sib(n).start()
        if n > 0:
            dispatch(n - 1)
    dispatch(CHUNKS - 1)
    pending.append(functools.partial(slots_sent, *there))

    use(13)
    use(14)
    slot_squares = 0.0
    for n in range(CHUNKS):
        slot_wait(n, *there)
        items = slots_in[n].reshape(n_ctx * slot_room, span)
        product = dot(items, gate_up[cols(n), :])
        slot_squares = slot_squares + square_sum(items, n)
        if n == 0:
            up_acc[...] = product
        else:
            up_acc[...] = up_acc[...] + product
    inner = down.shape[0]
    factor = norm_factor(slot_squares)
    gate_part = up_acc[:, :inner] * factor
    up_part = up_acc[:, inner:] * factor
    expert_hidden = (gate_part / (1.0 + jnp.exp(-gate_part)) * up_part).astype(BF16)
    for n in range(CHUNKS):
        result = dot(expert_hidden, down[:, cols(n)]).astype(BF16)
        back_out[n] = result.reshape(n_ctx, slot_room, span)
        loop(1, n_ctx, lambda d: slot_copy(n, d, *back).start())
        back_in[n, c] = back_out[n, c]
    pending.append(functools.partial(slots_sent, *back))

    use(10)
    use(11)
    group_squares = 0.0
    gate_sum = 0.0
    up_sum = 0.0
    for n in range(CHUNKS):
        block = normed[n].reshape(group, span)
        group_squares = group_squares + square_sum(block, n)
        gate_sum = gate_sum + dot_rows(block, shared_gate[:, cols(n)])
        up_sum = up_sum + dot_rows(block, shared_up[:, cols(n)])
    factor = norm_factor(group_squares)
    gate_part = gate_sum * factor
    up_part = up_sum * factor
    shared_hidden = (gate_part / (1.0 + jnp.exp(-gate_part)) * up_part).astype(BF16)
    use(12)

    give_rows = give[...].reshape(n_ctx * slot_room, group).astype(F32).T.astype(BF16)
    second = (part2, sib_in2, row_in2, b_sib_send, b_sib_recv, b_row_send, b_row_recv)
    for n in range(CHUNKS):
        slot_wait(n, *back)
        returned = back_in[n].reshape(n_ctx * slot_room, span)
        both = dot(shared_hidden, shared_down[:, cols(n)]) + dot(give_rows, returned)
        part2[n] = both.astype(BF16).reshape(2, n_chip, rows, span)
        sib_part(n, part2, sib_in2, b_sib_send, b_sib_recv).start()
        if n > 0:
            pass_rows(n - 1, *second)
    pass_rows(CHUNKS - 1, *second)
    pending.append(functools.partial(rows_sent, *second))
    for n in range(CHUNKS):
        out_ref[:, cols(n)] = (
            hidden[:, cols(n)] + sum_rows(n, row_in2, b_row_send, b_row_recv)
        )

    finish()


def shards(
    n_ctx,
    n_tp,
    queries,
    kv_latent,
    key_rope,
    w_key,
    w_value,
    w_out,
    residual,
    moe_gain,
    shared_gate,
    shared_up,
    shared_down,
    expert_gate_up,
    expert_down,
    expert_ids,
    gate_weights,
):
    rows, width = residual.shape
    n_chip = n_tp // 2
    heads = w_key.shape[1] // NOPE
    group = rows * n_tp
    latent = kv_latent.shape[1]
    slot_room = CAP * n_tp
    dma = pltpu.SemaphoreType.DMA
    scratch = [
        pltpu.VMEM(kv_latent.shape, BF16),
        pltpu.VMEM(key_rope.shape, BF16),
        pltpu.VMEM(expert_ids.shape[::-1], jnp.int32),
        pltpu.VMEM(gate_weights.shape[::-1], F32),
        pltpu.VMEM(queries.shape, BF16),
        pltpu.VMEM(w_key.shape, BF16),
        pltpu.VMEM(w_value.shape, BF16),
        pltpu.VMEM(residual.shape, BF16),
        pltpu.VMEM(moe_gain.shape, F32),
        pltpu.VMEM(w_out.shape, BF16),
        pltpu.VMEM(shared_gate.shape[::-1], BF16),
        pltpu.VMEM(shared_up.shape[::-1], BF16),
        pltpu.VMEM(shared_down.shape, BF16),
        pltpu.VMEM(expert_gate_up.shape[1:], BF16),
        pltpu.VMEM(expert_down.shape[1:], BF16),
        dma((15,)),
        pltpu.VMEM((n_ctx, 2, n_chip, rows, latent + 128), BF16),
        pltpu.VMEM((heads, group, 2 * NOPE), BF16),
        pltpu.VMEM((group, heads * NOPE), BF16),
        pltpu.VMEM((group, heads * VDIM), BF16),
        pltpu.VMEM((heads, group, 128), F32),
        pltpu.VMEM((heads, group, 2 * VDIM), F32),
        dma((n_ctx,)),
        dma((n_ctx,)),
        dma((n_ctx,)),
        dma((n_ctx,)),
        dma((n_ctx,)),
        dma((n_ctx,)),
        pltpu.VMEM((CHUNKS, 2, n_chip, rows, width // CHUNKS), BF16),
        pltpu.VMEM((CHUNKS, n_chip, rows, width // CHUNKS), BF16),
        pltpu.VMEM((CHUNKS, n_chip, rows, width // CHUNKS), BF16),
        dma((1,)),
        dma((CHUNKS,)),
        dma((1,)),
        dma((CHUNKS,)),
        pltpu.VMEM((rows, width), F32),
        pltpu.VMEM((CHUNKS, 2, n_chip, rows, width // CHUNKS), BF16),
        dma((1,)),
        dma((CHUNKS,)),
        dma((1,)),
        dma((CHUNKS,)),
        pltpu.VMEM((n_ctx, slot_room, group), BF16),
        pltpu.VMEM((n_ctx, slot_room, group), BF16),
        pltpu.VMEM((CHUNKS, n_ctx, slot_room, width // CHUNKS), BF16),
        pltpu.VMEM((CHUNKS, n_ctx, slot_room, width // CHUNKS), BF16),
        pltpu.VMEM((n_ctx * slot_room, expert_gate_up.shape[2]), F32),
        dma((1,)),
        dma((CHUNKS,)),
        pltpu.VMEM((CHUNKS, n_ctx, slot_room, width // CHUNKS), BF16),
        pltpu.VMEM((CHUNKS, n_ctx, slot_room, width // CHUNKS), BF16),
        dma((1,)),
        dma((CHUNKS,)),
        pltpu.VMEM((CHUNKS, 2, n_chip, rows, width // CHUNKS), BF16),
        pltpu.VMEM((CHUNKS, n_chip, rows, width // CHUNKS), BF16),
        pltpu.VMEM((CHUNKS, n_chip, rows, width // CHUNKS), BF16),
        dma((1,)),
        dma((CHUNKS,)),
        dma((1,)),
        dma((CHUNKS,)),
    ]
    vmem = pl.BlockSpec(memory_space=pltpu.VMEM)
    hbm = pl.BlockSpec(memory_space=pl.ANY)
    return pl.pallas_call(
        layer_kernel,
        out_shape=jax.ShapeDtypeStruct((rows, width), F32),
        in_specs=[hbm] * 15,
        out_specs=vmem,
        scratch_shapes=scratch,
        compiler_params=pltpu.CompilerParams(
            collective_id=1, has_side_effects=True, vmem_limit_bytes=63 * 1024 * 1024
        ),
        cost_estimate=pl.CostEstimate(
            flops=20_000_000_000, bytes_accessed=20_000_000, transcendentals=9_000_000
        ),
        name="layer",
    )(
        queries,
        kv_latent,
        key_rope,
        w_key,
        w_value,
        w_out,
        residual,
        moe_gain,
        shared_gate.T,
        shared_up.T,
        shared_down,
        expert_gate_up,
        expert_down,
        expert_ids.T,
        gate_weights.T,
    ).astype(BF16)


def solution(mesh):
    in_specs = (
        P("ctx", "tp"),
        P(("ctx", "tp"), None),
        P(("ctx", "tp"), None),
        P(None, "tp"),
        P(None, "tp"),
        P("tp", None),
        P(("ctx", "tp"), None),
        P(),
        P(None, "tp"),
        P(None, "tp"),
        P("tp", None),
        P(("ctx", "tp"), None, None),
        P(("ctx", "tp"), None, None),
        P(("ctx", "tp"), None),
        P(("ctx", "tp"), None),
    )
    out_specs = P(("ctx", "tp"), None)
    return jax.shard_map(
        functools.partial(shards, mesh.shape["ctx"], mesh.shape["tp"]),
        mesh=mesh,
        in_specs=in_specs,
        out_specs=out_specs,
        check_vma=False,
    )
```
